32 devices in a mesh: snd: 8 (over z, y), map: 4 (over x, core).
Axes of the slice: x: 2, y: 2, z: 4, core: 2. Of those that a mesh axis runs over, the one named last changes fastest.
Arguments:
- sensitivity_blocks: bfloat16 [4096, 128, 128], P(('snd', 'map')), may hold values from -0.1875 to 0.1875
- block_placement_table: int32 [3, 4096], P(None, ('snd', 'map')), may hold values from 0 to 63, as said below
- needed_tile_lists: int32 [256, 4], P(('snd', 'map')), may hold values from -1 to 127, as said below
- location_category: int32 [32768], P('map'), may hold values from 0 to 15
- ground_warmth_celsius: float32 [16, 32768], P('snd', 'map'), may hold values from -5 to 30
- wetness_factor: float32 [16, 32768], P('snd', 'map'), may hold values from 0.2 to 1
- carbon_reservoirs: float32 [3, 32768], P(None, 'map'), may hold values from 0.2 to 3
- category_sensitivity_effect: float32 [16], replicated, may hold values from -4 to 4
- reservoir_decay_effect: float32 [3, 16], replicated, may hold values from -4 to 4
- measured_anomaly: float32 [512, 128], P(('snd', 'map')), may hold values from -6 to 6
- retrieval_precision: float32 [512, 128], P(('snd', 'map')), may hold values from 0.5 to 2
Outputs:
- model_xco2: float32 [512, 128], P(('snd', 'map'))
- flux_grad: float32 [16, 32768], P('snd', 'map')
- class_grad: float32 [4, 16], replicated
- cost: float32 [], replicated
The draws below stay inside these ranges and needn't reach their ends.
Inputs may be any that keep to these rules, and one draw needn't show every extreme that they name: `block_placement_table`: row 0 is a block row below 64, row 1 a cell tile below 64, row 2 a slot below 16; each block's tile appears in its device's request list to the owner of its slot (slot // 2) as (slot % 2) * 64 + tile. `needed_tile_lists`: row o of a device's 8 rows lists distinct local tile ids of owner o followed by -1; every list has 1 to 4 ids, and on every device some list has exactly 4.
All inputs are finite; a program needn't handle non-finite values.
Results may differ from the reference program's by a relative error of at most 0.0039.
Values may be sent and summed in bfloat16 or wider, within the bound.
A program may use at most 64 MiB of HBM per device.

```python
import math
import jax
import jax.numpy as jnp
from jax import lax

TILE = 128
NCLASS = 16
CAP = 4
SLOT_DEV = 2
CT_DEV = 64
BR_DEV = 64
NB_DEV = 128
EPOCH_NUMBER = 16
MAP_LOCATIONS = 32768
SROWS = 512
NBLK = 4096
N_SND = 8
N_MAP = 4


def plan_tables(key):

    def single(dev_key):
        count_key, perm_key, row_key, full_key = jax.random.split(dev_key, 4)
        counts = jax.random.randint(count_key, (N_SND,), 1, CAP + 1)
        fullest = jax.random.randint(full_key, (), 0, N_SND)
        counts = jnp.where(jnp.arange(N_SND, dtype=jnp.int32) == fullest, CAP, counts).astype(jnp.int32)
        perm_keys = jax.random.split(perm_key, N_SND)
        orders = jax.vmap(lambda k: jax.random.permutation(k, SLOT_DEV * CT_DEV))(perm_keys).astype(jnp.int32)
        top_id = SLOT_DEV * CT_DEV - 1
        turned = (orders - orders[:, :1] + top_id) % (SLOT_DEV * CT_DEV)
        last_row = (jnp.arange(N_SND, dtype=jnp.int32) == N_SND - 1)[:, None]
        orders = jnp.where(last_row, turned, orders).astype(jnp.int32)
        chosen = orders[:, :CAP]
        live = jnp.arange(CAP, dtype=jnp.int32)[None, :] < counts[:, None]
        lists = jnp.where(live, chosen, -1)
        ends = jnp.cumsum(counts)
        total = ends[-1]
        flat = jnp.arange(NB_DEV, dtype=jnp.int32) % total
        owner = jnp.sum((ends[None, :] <= flat[:, None]).astype(jnp.int32), axis=1)
        starts = ends - counts
        within = flat - starts[owner]
        local_id = chosen[owner, within]
        slot = owner * SLOT_DEV + local_id // CT_DEV
        tile_id = local_id % CT_DEV
        rows = jax.random.randint(row_key, (NB_DEV,), 0, BR_DEV).astype(jnp.int32)
        rows = jnp.where(jnp.arange(NB_DEV, dtype=jnp.int32) == 0, BR_DEV - 1, rows).astype(jnp.int32)
        return (jnp.stack([rows, tile_id, slot]), lists)
    keys = jax.random.split(jax.random.fold_in(key, 7), N_SND * N_MAP)
    cover, lists = jax.vmap(single)(keys)
    return (cover.transpose(1, 0, 2).reshape(3, N_SND * N_MAP * NB_DEV), lists.reshape(N_SND * N_MAP * N_SND, CAP))


def draw_block_placement_table(key, part):
    return plan_tables(key)[0]


def draw_needed_tile_lists(key, part):
    return plan_tables(key)[1]


def place_ends(drawn, key, least, high):
    index_at = [jax.random.randint(jax.random.fold_in(key, axis), (), 0, length) for axis, length in enumerate(drawn.shape)]
    main_axis = drawn.shape.index(max(drawn.shape))
    beside = index_at[:main_axis] + [(index_at[main_axis] + 1) % drawn.shape[main_axis]] + index_at[main_axis + 1:]
    return drawn.at[tuple(index_at)].set(least).at[tuple(beside)].set(high)


def block_levels(stream_key, dims, shards, low, largest):
    gain, own = 1.0, jax.random.fold_in(stream_key, 6)
    for dim, shards_of in shards:
        heights = jnp.exp(jax.random.uniform(jax.random.fold_in(own, dim), (shards_of,), jnp.float32, low / len(shards), largest / len(shards)))
        gain = gain * jnp.repeat(heights, dims[dim] // shards_of).reshape([-1 if axis == dim else 1 for axis in range(len(dims))])
    return gain


def centred(rng, dims, width, most, cuts=(), kind=jnp.bfloat16):
    factor_of = block_levels(rng, dims, cuts, -0.22, 0.18) if cuts else 1.0
    values = jax.random.normal(rng, dims, jnp.float32) * width * factor_of
    return jnp.minimum(jnp.maximum(values, -most), most).astype(kind)


def setup_inputs(seed: int = 0) -> dict:
    key_of = jax.random.split(jax.random.key(seed), 12)
    return {
        "sensitivity_blocks": centred(key_of[0], (NBLK, TILE, TILE), (NB_DEV * N_MAP * TILE // BR_DEV) ** -0.5, 0.1875, ((0, 32),)),
        "block_placement_table": draw_block_placement_table(jax.random.fold_in(key_of[11], 71), 0),
        "needed_tile_lists": draw_needed_tile_lists(jax.random.fold_in(key_of[11], 71), 0),
        "location_category": place_ends(jax.random.randint(key_of[3], (MAP_LOCATIONS,), 0, NCLASS), jax.random.fold_in(key_of[3], 1), 0, NCLASS - 1).astype(jnp.int32),
        "ground_warmth_celsius": jnp.clip(-5.0 + 35.0 * jax.random.uniform(key_of[4], (EPOCH_NUMBER, MAP_LOCATIONS), jnp.float32) ** block_levels(key_of[4], (EPOCH_NUMBER, MAP_LOCATIONS), ((0, 8), (1, 4)), -0.2, 0.2), -5.0, 30.0),
        "wetness_factor": jnp.clip(0.2 + 0.8 * jax.random.uniform(key_of[5], (EPOCH_NUMBER, MAP_LOCATIONS), jnp.float32) ** block_levels(key_of[5], (EPOCH_NUMBER, MAP_LOCATIONS), ((0, 8), (1, 4)), -0.2, 0.2), 0.2, 1.0),
        "carbon_reservoirs": jnp.clip(jnp.exp(math.log(3.0) - 2.7080502 * jax.random.uniform(key_of[6], (3, MAP_LOCATIONS), jnp.float32) ** block_levels(key_of[6], (3, MAP_LOCATIONS), ((1, 4),), -0.2, 0.2)), 0.2, 3.0),
        "category_sensitivity_effect": centred(key_of[7], (NCLASS,), 0.3, 4.0, (), jnp.float32),
        "reservoir_decay_effect": centred(key_of[8], (3, NCLASS), 0.3, 4.0, (), jnp.float32),
        "measured_anomaly": centred(key_of[9], (SROWS, TILE), 1.0, 6.0, ((0, 32),), jnp.float32),
        "retrieval_precision": jnp.clip(jnp.exp(math.log(2.0) - 1.3862944 * jax.random.uniform(key_of[10], (SROWS, TILE), jnp.float32) ** block_levels(key_of[10], (SROWS, TILE), ((0, 32),), -0.2, 0.2)), 0.5, 2.0),
    }


BASELINE_CELSIUS = 15.0
LOG_BASE_Q = 0.6931471805599453
PRIOR_VAR = 0.09


def ground_efflux_forward(ground_warmth_celsius, wetness_factor, carbon_reservoirs, location_category, category_sensitivity_effect, reservoir_decay_effect):
    nclass = category_sensitivity_effect.shape[0]
    category_onehot = (location_category[None, :] == jnp.arange(nclass, dtype=jnp.int32)[:, None]).astype(jnp.float32)
    log_q = LOG_BASE_Q + jnp.dot(category_sensitivity_effect[None, :], category_onehot, precision=lax.Precision.HIGHEST)[0]
    base = jnp.array([0.6, 0.25, 0.1], dtype=jnp.float32)
    rates = base[:, None] * jnp.exp(jnp.dot(reservoir_decay_effect, category_onehot, precision=lax.Precision.HIGHEST))
    decay_lifetime = (ground_warmth_celsius - BASELINE_CELSIUS) / 10.0
    modifier = jnp.exp(log_q[None, :] * decay_lifetime) * wetness_factor
    device_number = (rates * carbon_reservoirs)[:, None, :] * modifier[None]
    return category_onehot, decay_lifetime, device_number


def reference(sensitivity_blocks, block_placement_table, needed_tile_lists, location_category, ground_warmth_celsius, wetness_factor, carbon_reservoirs, category_sensitivity_effect, reservoir_decay_effect, measured_anomaly, retrieval_precision):
    category_onehot, decay_lifetime, device_number = ground_efflux_forward(ground_warmth_celsius, wetness_factor, carbon_reservoirs, location_category, category_sensitivity_effect, reservoir_decay_effect)
    flux = device_number[0] + device_number[1] + device_number[2]
    tiles = flux.astype(jnp.bfloat16).reshape(EPOCH_NUMBER, N_MAP, CT_DEV, TILE)
    ndevs = N_SND * N_MAP
    blocks = sensitivity_blocks.reshape(ndevs, NB_DEV, TILE, TILE)
    cover = block_placement_table.reshape(3, ndevs, NB_DEV).transpose(1, 0, 2)
    devs = jnp.arange(ndevs, dtype=jnp.int32)

    def forward(carry, item):
        dev, blk, cov = item
        group = dev % N_MAP
        vectors = tiles[cov[2], group, cov[1]]
        contrib = jnp.einsum('bij,bj->bi', blk.astype(jnp.float32), vectors.astype(jnp.float32))
        rows = (dev // N_MAP) * BR_DEV + cov[0]
        return carry.at[rows].add(contrib), None

    model_xco2, _ = lax.scan(forward, jnp.zeros((SROWS, TILE), jnp.float32), (devs, blocks, cover))
    diff = model_xco2 - measured_anomaly
    weighted = (diff * retrieval_precision).astype(jnp.bfloat16)

    def adjoint(carry, item):
        dev, blk, cov = item
        group = dev % N_MAP
        rows = (dev // N_MAP) * BR_DEV + cov[0]
        back = weighted[rows].astype(jnp.float32)
        grads = jnp.einsum('bij,bi->bj', blk.astype(jnp.float32), back)
        return carry.at[cov[2], group, cov[1]].add(grads), None

    grad_tiles, _ = lax.scan(adjoint, jnp.zeros((EPOCH_NUMBER, N_MAP, CT_DEV, TILE), jnp.float32), (devs, blocks, cover))
    flux_grad = grad_tiles.reshape(EPOCH_NUMBER, MAP_LOCATIONS)
    terms = jnp.stack([jnp.sum(flux_grad * flux * decay_lifetime, axis=0), jnp.sum(flux_grad * device_number[0], axis=0), jnp.sum(flux_grad * device_number[1], axis=0), jnp.sum(flux_grad * device_number[2], axis=0)])
    class_part = jnp.dot(terms, category_onehot.T, precision=lax.Precision.HIGHEST)
    prior = jnp.concatenate([category_sensitivity_effect[None, :], reservoir_decay_effect], axis=0) / PRIOR_VAR
    class_grad = class_part + prior
    cost = 0.5 * jnp.sum(retrieval_precision * diff * diff) + 0.5 * jnp.sum(category_sensitivity_effect * category_sensitivity_effect) / PRIOR_VAR + 0.5 * jnp.sum(reservoir_decay_effect * reservoir_decay_effect) / PRIOR_VAR
    return model_xco2, flux_grad, class_grad, cost
```

```python
import functools

import jax
import jax.numpy as jnp
from jax import lax
from jax.experimental import pallas as pl
from jax.experimental.pallas import tpu as pltpu
from jax.sharding import PartitionSpec as P

BASELINE_CELSIUS = 15.0
LOG_BASE_Q = 0.6931471805599453
PRIOR_VAR = 0.09
RATES = (0.6, 0.25, 0.1)
CHUNK = 8
F32 = jnp.float32
BF16 = jnp.bfloat16


def split3(x):
    hi = x.astype(BF16)
    rest = x - hi.astype(F32)
    mid = rest.astype(BF16)
    low = (rest - mid.astype(F32)).astype(BF16)
    return hi, mid, low


def dot(a, b, dims):
    return lax.dot_general(a, b, (dims, ((), ())), preferred_element_type=F32)


def onehot(mask):
    return jnp.where(mask, 1.0, 0.0).astype(BF16)


def pick(sel, x):
    hi, mid, low = split3(x)
    return (dot(sel, hi, ((1,), (0,))) + dot(sel, mid, ((1,), (0,)))) + dot(sel, low, ((1,), (0,)))


def iota(shape, dim):
    return lax.broadcasted_iota(jnp.int32, shape, dim)


def kernel(
    n_s, n_m, sens_hbm, table, lists, cat_hbm, warm_hbm, wet_hbm, carb_hbm, q_s, r_s, q_v, r_v, meas_hbm, prec_hbm,
    model_out, grad_out, class_out, cost_out,
    sens, cat, warm_in, wet_in, carb_in, warm, wet, carb,
    req_send, req_recv, rep_send, rep_recv, mbuf, part, gsend, grecv, tsend, trecv,
    ids, vecs, tcol, rcol, model, fg, srows,
    local_sem, s_req, r_req, s_rep, r_rep, s_m, r_m, s_p, r_p, s_g, r_g, s_t, r_t,
):
    cap = lists.shape[1]
    nreq = n_s * cap
    slots = warm_hbm.shape[0]
    tiles = cat.shape[0]
    nclass = q_s.shape[0]
    pools = carb_hbm.shape[0]
    rows = meas_hbm.shape[0]
    allrows = rows * n_m
    nb = table.shape[1]
    tile = sens.shape[1]
    me = lax.axis_index("snd")
    mm = lax.axis_index("map")
    snd_dev = lambda e: {"snd": lax.rem(me + e + n_s, n_s)}
    map_dev = lambda f: {"map": lax.rem(mm + f + n_m, n_m)}

    def remote(src, dst, ss, rs, dev):
        return pltpu.make_async_remote_copy(
            src_ref=src, dst_ref=dst, send_sem=ss, recv_sem=rs, device_id=dev, device_id_type=pl.DeviceIdType.MESH
        )

    barrier = pltpu.get_barrier_semaphore()
    for e in range(1, n_s):
        pl.semaphore_signal(barrier, inc=1, device_id=snd_dev(e), device_id_type=pl.DeviceIdType.MESH)
    for f in range(1, n_m):
        pl.semaphore_signal(barrier, inc=1, device_id=map_dev(f), device_id_type=pl.DeviceIdType.MESH)

    loads = [
        pltpu.make_async_copy(src, dst, local_sem.at[i])
        for i, (src, dst) in enumerate(
            [
                (warm_hbm, warm_in),
                (wet_hbm, wet_in),
                (carb_hbm, carb_in),
                (cat_hbm, cat),
                (meas_hbm, mbuf.at[0, 0]),
                (prec_hbm, mbuf.at[0, 1]),
                (sens_hbm, sens),
            ]
        )
    ]
    for load in loads:
        load.start()

    row_in = iota((cap, tile), 0)
    for e in range(n_s):
        owner = lax.rem(me + e, n_s)
        whole_id = jnp.full((cap, tile), -1, jnp.int32)
        spot = jnp.full((cap, tile), -1, jnp.int32)
        tile_id = jnp.full((cap, tile), -1, jnp.int32)
        for k in range(cap):
            asked = lists[owner, k]
            t = lax.rem(asked, tiles)
            here = row_in == k
            whole_id = jnp.where(here, jnp.where(asked < 0, -1, owner * (slots * tiles) + asked), whole_id)
            spot = jnp.where(here, t * slots + lax.div(asked, tiles), spot)
            tile_id = jnp.where(here, t, tile_id)
        if e == 0:
            req_recv[0] = spot
        else:
            req_send[e] = spot
        ids[0, pl.ds(e * cap, cap), :] = whole_id
        ids[1, pl.ds(e * cap, cap), :] = tile_id

    pl.semaphore_wait(barrier, n_s - 1 + n_m - 1)

    req = [remote(req_send.at[e], req_recv.at[e], s_req.at[e], r_req.at[e], snd_dev(e)) for e in range(1, n_s)]
    for c in req:
        c.start()
    obs = []
    for f in range(1, n_m):
        obs.append(remote(meas_hbm, mbuf.at[f, 0], s_m.at[f, 0], r_m.at[f, 0], map_dev(f)))
        obs.append(remote(prec_hbm, mbuf.at[f, 1], s_m.at[f, 1], r_m.at[f, 1], map_dev(f)))
    for c in obs:
        c.start()

    carb[...] = jnp.zeros_like(carb)
    for load in loads[:4]:
        load.wait()
    for t in range(tiles):
        lanes = pl.ds(t * tile, tile)
        warm[pl.ds(slots * t, slots), :] = warm_in[:, lanes]
        wet[pl.ds(slots * t, slots), :] = wet_in[:, lanes]
        carb[pl.ds(4 * t, pools), :] = carb_in[:, lanes]
    warm_parts = split3(warm[...])
    wet_parts = split3(wet[...])

    tile_id = ids[1]
    cls = dot(onehot(tile_id[:, :tiles] == iota((nreq, tiles), 1)), cat[...].astype(F32).astype(BF16), ((1,), (0,)))
    cls = cls.astype(jnp.int32)
    wide = jnp.concatenate([tile_id] * (4 * tiles // tile), axis=1)
    wide_at = iota((nreq, 4 * tiles), 1)
    log_q = jnp.zeros((nreq, tile), F32)
    effects = [jnp.zeros((nreq, tile), F32) for _ in range(pools)]
    for c in range(nclass):
        here = cls == c
        log_q = jnp.where(here, q_s[c], log_q)
        for p in range(pools):
            effects[p] = jnp.where(here, r_s[p, c], effects[p])
    log_q = LOG_BASE_Q + log_q
    held = []
    for p in range(pools):
        carbon = pick(onehot(wide * 4 + p == wide_at), carb[...])
        held.append(RATES[p] * jnp.exp(effects[p]) * carbon)

    block_row = table[0:1, :]
    block_id = table[2:3, :] * tiles + table[1:2, :]
    asked_hot = onehot(ids[0][:, :nb] == block_id)
    row_hot = onehot(iota((allrows, nb), 0) == block_row)
    tcol[...] = dot(asked_hot, iota((nreq, tile), 0).astype(F32).astype(BF16), ((0,), (0,)))
    rcol[...] = dot(row_hot, iota((allrows, tile), 0).astype(F32).astype(BF16), ((0,), (0,)))

    for c in req:
        c.wait_recv()
    for e in range(n_s):
        ids[0, pl.ds(e * cap, cap), :] = req_recv[e]
    sel = onehot(ids[0] == iota((nreq, tile), 1))
    every = dot(sel, jnp.concatenate(list(warm_parts) + list(wet_parts), axis=1), ((1,), (0,)))
    cut = [every[:, i * tile : (i + 1) * tile] for i in range(6)]
    out_warm = (cut[0] + cut[1]) + cut[2]
    out_wet = (cut[3] + cut[4]) + cut[5]
    rep = []
    for e in range(n_s):
        to = rep_recv if e == 0 else rep_send
        to[e, 0:cap, :] = out_warm[e * cap : (e + 1) * cap]
        to[e, cap : 2 * cap, :] = out_wet[e * cap : (e + 1) * cap]
        if e:
            rep.append(remote(rep_send.at[e], rep_recv.at[e], s_rep.at[e], r_rep.at[e], snd_dev(-e)))
            rep[-1].start()
    for c in rep:
        c.wait_recv()
    for e in range(n_s):
        vecs[0, pl.ds(e * cap, cap), :] = rep_recv[e, 0:cap, :]
        vecs[1, pl.ds(e * cap, cap), :] = rep_recv[e, cap : 2 * cap, :]

    tau = (vecs[0] - BASELINE_CELSIUS) / 10.0
    modifier = jnp.exp(log_q * tau) * vecs[1]
    pieces = [h * modifier for h in held]
    flux = pieces[0] + pieces[1] + pieces[2]
    flux_low = flux.astype(BF16)

    tcol_hot = onehot(tcol[:, :nreq] == iota((nb, nreq), 1).astype(F32))
    vecs_b = dot(tcol_hot, flux_low, ((1,), (0,)))
    model_at = iota((allrows, tile), 0).astype(F32)
    vb = fg
    vb[...] = vecs_b
    loads[6].wait()

    def forward(step, acc):
        at = pl.multiple_of(step * CHUNK, CHUNK)
        v = vb[pl.ds(at, CHUNK), :]
        r = rcol[pl.ds(at, CHUNK), :]
        left = [jnp.where(model_at == r[u : u + 1], v[u : u + 1], 0.0).astype(BF16) for u in range(CHUNK)]
        right = [
            sens[pl.ds(pl.multiple_of((step * CHUNK + u) * tile, tile), tile), :] for u in range(CHUNK)
        ]
        return acc + dot(jnp.concatenate(left, axis=1), jnp.concatenate(right, axis=1), ((1,), (1,)))

    part[0] = lax.fori_loop(0, nb // CHUNK, forward, jnp.zeros((allrows, tile), F32))

    swap = [remote(part.at[0], part.at[f], s_p.at[f], r_p.at[f], map_dev(f)) for f in range(1, n_m)]
    for c in swap:
        c.start()
    for c in loads[4:6]:
        c.wait()
    for c in obs:
        c.wait_recv()
    meas, prec = [], []
    for a in range(n_m):
        slot = lax.rem(mm - a + n_m, n_m)
        meas.append(mbuf[slot, 0])
        prec.append(mbuf[slot, 1])
    meas = jnp.concatenate(meas, axis=0)
    prec = jnp.concatenate(prec, axis=0)
    rcol_hot = onehot(rcol[:, :allrows] == iota((nb, allrows), 1).astype(F32))
    for c in swap:
        c.wait_recv()
    total = part[lax.rem(mm + n_m, n_m)]
    for a in range(1, n_m):
        total = total + part[lax.rem(mm - a + n_m, n_m)]
    model[...] = total
    diff = total - meas
    weighted = (diff * prec).astype(BF16)
    own = model[pl.ds(pl.multiple_of(mm * rows, rows), rows), :]
    model_out[...] = own
    own_diff = own - mbuf[0, 0]
    misfit = 0.5 * jnp.sum(mbuf[0, 1] * own_diff * own_diff, keepdims=True)

    vb[...] = dot(rcol_hot, weighted, ((1,), (0,)))
    asked_at = iota((nreq, tile), 0).astype(F32)

    def backward(step, acc):
        at = pl.multiple_of(step * CHUNK, CHUNK)
        v = vb[pl.ds(at, CHUNK), :]
        r = tcol[pl.ds(at, CHUNK), :]
        left = [jnp.where(asked_at == r[u : u + 1], v[u : u + 1], 0.0).astype(BF16) for u in range(CHUNK)]
        right = sens[pl.ds(pl.multiple_of(step * CHUNK * tile, CHUNK * tile), CHUNK * tile), :]
        return acc + dot(jnp.concatenate(left, axis=1), right, ((1,), (0,)))

    grads = lax.fori_loop(0, nb // CHUNK, backward, jnp.zeros((nreq, tile), F32))

    terms = [grads * flux * tau] + [grads * piece for piece in pieces]
    for c in range(nclass):
        here = cls == c
        for p, term in enumerate(terms):
            srows[pl.ds(p * nclass + c, 1), :] = jnp.sum(jnp.where(here, term, 0.0), axis=0, keepdims=True)
    sums = jnp.sum(srows[...], axis=1, keepdims=True)
    diagonal = iota((nclass, tile), 0) == iota((nclass, tile), 1)
    lines = []
    for p in range(1 + pools):
        line = jnp.sum(jnp.where(diagonal, sums[p * nclass : (p + 1) * nclass], 0.0), axis=0, keepdims=True)
        if p == 0:
            line = jnp.where(iota((1, tile), 1) == nclass, misfit, line)
        lines.append(line)
    share = jnp.concatenate(lines, axis=0)
    back = []
    for e in range(n_s):
        to = grecv if e == 0 else gsend
        to[e, 0:cap, :] = grads[e * cap : (e + 1) * cap]
        to[e, cap:, :] = share
        if e:
            back.append(remote(gsend.at[e], grecv.at[e], s_g.at[e], r_g.at[e], snd_dev(e)))
            back[-1].start()
    for c in back:
        c.wait_recv()
    share = grecv[0, cap:, :]
    for e in range(1, n_s):
        share = share + grecv[e, cap:, :]
    trecv[0] = share
    last = [remote(trecv.at[0], trecv.at[f], s_t.at[f], r_t.at[f], map_dev(f)) for f in range(1, n_m)]
    for c in last:
        c.start()

    for e in range(n_s):
        vecs[0, pl.ds(e * cap, cap), :] = grecv[e, 0:cap, :]
    hi, mid, low = split3(vecs[0])
    placed = (dot(sel, hi, ((0,), (0,))) + dot(sel, mid, ((0,), (0,)))) + dot(sel, low, ((0,), (0,)))
    fg[...] = placed
    for t in range(tiles):
        grad_out[:, pl.ds(t * tile, tile)] = fg[pl.ds(slots * t, slots), :]

    for c in last:
        c.wait_recv()
    share = trecv[lax.rem(mm + n_m, n_m)]
    for a in range(1, n_m):
        share = share + trecv[lax.rem(mm - a + n_m, n_m)]
    class_out[0:1, :] = share[0:1, :nclass] + q_v[...] / PRIOR_VAR
    class_out[1:, :] = share[1:, :nclass] + r_v[...] / PRIOR_VAR
    prior = jnp.sum(q_v[...] * q_v[...], keepdims=True) + jnp.sum(r_v[...] * r_v[...], keepdims=True)
    cost_out[...] = share[0:1, nclass : nclass + 1] + 0.5 * prior / PRIOR_VAR

    for c in req + obs + rep + swap + back + last:
        c.wait_send()


def shards(
    n_s,
    n_m,
    sensitivity_blocks,
    block_placement_table,
    needed_tile_lists,
    location_category,
    ground_warmth_celsius,
    wetness_factor,
    carbon_reservoirs,
    category_sensitivity_effect,
    reservoir_decay_effect,
    measured_anomaly,
    retrieval_precision,
):
    nb, tile, _ = sensitivity_blocks.shape
    slots, cells = ground_warmth_celsius.shape
    pools, nclass = reservoir_decay_effect.shape
    tiles = cells // tile
    cap = needed_tile_lists.shape[1]
    nreq = n_s * cap
    rows = measured_anomaly.shape[0]
    allrows = rows * n_m
    hbm = pl.BlockSpec(memory_space=pl.ANY)
    vmem = pl.BlockSpec(memory_space=pltpu.VMEM)
    smem = pl.BlockSpec(memory_space=pltpu.SMEM)
    sem = pltpu.SemaphoreType.DMA
    blocks = nb * tile
    model, grad, classes, cost = pl.pallas_call(
        functools.partial(kernel, n_s, n_m),
        out_shape=(
            jax.ShapeDtypeStruct((rows, tile), F32),
            jax.ShapeDtypeStruct((slots, cells), F32),
            jax.ShapeDtypeStruct((1 + pools, nclass), F32),
            jax.ShapeDtypeStruct((1, 1), F32),
        ),
        in_specs=[hbm, vmem, smem, hbm, hbm, hbm, hbm, smem, smem, vmem, vmem, hbm, hbm],
        out_specs=(vmem, vmem, vmem, vmem),
        scratch_shapes=[
            pltpu.VMEM((blocks, tile), BF16),
            pltpu.VMEM((tiles, tile), jnp.int32),
            pltpu.VMEM((slots, cells), F32),
            pltpu.VMEM((slots, cells), F32),
            pltpu.VMEM((pools, cells), F32),
            pltpu.VMEM((tiles * slots, tile), F32),
            pltpu.VMEM((tiles * slots, tile), F32),
            pltpu.VMEM((tiles * 4, tile), F32),
            pltpu.VMEM((n_s, cap, tile), jnp.int32),
            pltpu.VMEM((n_s, cap, tile), jnp.int32),
            pltpu.VMEM((n_s, 2 * cap, tile), F32),
            pltpu.VMEM((n_s, 2 * cap, tile), F32),
            pltpu.VMEM((n_m, 2, rows, tile), F32),
            pltpu.VMEM((n_m, allrows, tile), F32),
            pltpu.VMEM((n_s, cap + 1 + pools, tile), F32),
            pltpu.VMEM((n_s, cap + 1 + pools, tile), F32),
            pltpu.VMEM((1 + pools, tile), F32),
            pltpu.VMEM((n_m, 1 + pools, tile), F32),
            pltpu.VMEM((2, nreq, tile), jnp.int32),
            pltpu.VMEM((2, nreq, tile), F32),
            pltpu.VMEM((nb, tile), F32),
            pltpu.VMEM((nb, tile), F32),
            pltpu.VMEM((allrows, tile), F32),
            pltpu.VMEM((tiles * slots, tile), F32),
            pltpu.VMEM(((1 + pools) * nclass, tile), F32),
            sem((7,)),
            sem((n_s,)),
            sem((n_s,)),
            sem((n_s,)),
            sem((n_s,)),
            sem((n_m, 2)),
            sem((n_m, 2)),
            sem((n_m,)),
            sem((n_m,)),
            sem((n_s,)),
            sem((n_s,)),
            sem((n_m,)),
            sem((n_m,)),
        ],
        compiler_params=pltpu.CompilerParams(
            collective_id=0, has_side_effects=True, vmem_limit_bytes=24 * 1024 * 1024
        ),
        cost_estimate=pl.CostEstimate(
            flops=2 * blocks * tile * (allrows + nreq), bytes_accessed=2 * blocks * tile, transcendentals=4 * nreq * tile
        ),
        name="inversion",
    )(
        sensitivity_blocks.reshape(blocks, tile),
        block_placement_table,
        needed_tile_lists,
        location_category.reshape(tiles, tile),
        ground_warmth_celsius,
        wetness_factor,
        carbon_reservoirs,
        category_sensitivity_effect,
        reservoir_decay_effect,
        category_sensitivity_effect.reshape(1, nclass),
        reservoir_decay_effect,
        measured_anomaly,
        retrieval_precision,
    )
    return model, grad, classes, cost.reshape(())


def solution(mesh):
    in_specs = (
        P(("snd", "map"), None, None),
        P(None, ("snd", "map")),
        P(("snd", "map"), None),
        P("map"),
        P("snd", "map"),
        P("snd", "map"),
        P(None, "map"),
        P(),
        P(),
        P(("snd", "map"), None),
        P(("snd", "map"), None),
    )
    out_specs = (P(("snd", "map"), None), P("snd", "map"), P(), P())
    return jax.shard_map(
        functools.partial(shards, mesh.shape["snd"], mesh.shape["map"]),
        mesh=mesh,
        in_specs=in_specs,
        out_specs=out_specs,
        check_vma=False,
    )
```

```python
import functools

import jax
import jax.numpy as jnp
from jax import lax
from jax.experimental import pallas as pl
from jax.experimental.pallas import tpu as pltpu
from jax.sharding import PartitionSpec as P

BASELINE_CELSIUS = 15.0
LOG_BASE_Q = 0.6931471805599453
PRIOR_VAR = 0.09
RATES = (0.6, 0.25, 0.1)
CHUNK = 32
F32 = jnp.float32
BF16 = jnp.bfloat16


def split3(x):
    hi = x.astype(BF16)
    rest = x - hi.astype(F32)
    mid = rest.astype(BF16)
    low = (rest - mid.astype(F32)).astype(BF16)
    return hi, mid, low


def dot(a, b, dims):
    return lax.dot_general(a, b, (dims, ((), ())), preferred_element_type=F32)


def onehot(mask):
    return jnp.where(mask, 1.0, 0.0).astype(BF16)


def pick(sel, x):
    hi, mid, low = split3(x)
    return (dot(sel, hi, ((1,), (0,))) + dot(sel, mid, ((1,), (0,)))) + dot(sel, low, ((1,), (0,)))


def iota(shape, dim):
    return lax.broadcasted_iota(jnp.int32, shape, dim)


def kernel(
    n_s, n_m, sens_hbm, table_hbm, lists, cat_hbm, warm_hbm, wet_hbm, carb_hbm, q_s, r_s, q_hbm, r_hbm, meas_hbm,
    prec_hbm, model_hbm, grad_hbm, class_hbm, cost_hbm,
    model_out, grad_out, class_out, cost_out, table, q_v, r_v, vb, sens, cat, warm_in, wet_in, carb_in, warm, wet, carb,
    req_send, req_recv, rep_send, rep_recv, mbuf, part, gsend, grecv, tsend, trecv,
    ids, vecs, tcol, rcol, model, fg, srows,
    local_sem, out_sem, s_req, r_req, s_rep, r_rep, s_m, r_m, s_p, r_p, s_g, r_g, s_t, r_t,
):
    cap = lists.shape[0]
    nreq = n_s * cap
    slots = warm_hbm.shape[0]
    tiles = cat.shape[0]
    nclass = q_s.shape[0]
    pools = carb_hbm.shape[0]
    rows = meas_hbm.shape[0]
    allrows = rows * n_m
    nb = table.shape[1]
    tile = sens.shape[1]
    me = lax.axis_index("snd")
    mm = lax.axis_index("map")
    snd_dev = lambda e: {"snd": lax.rem(me + e + n_s, n_s)}
    map_dev = lambda f: {"map": lax.rem(mm + f + n_m, n_m)}

    def remote(src, dst, ss, rs, dev):
        return pltpu.make_async_remote_copy(
            src_ref=src, dst_ref=dst, send_sem=ss, recv_sem=rs, device_id=dev, device_id_type=pl.DeviceIdType.MESH
        )

    barrier = pltpu.get_barrier_semaphore()
    for e in range(1, n_s):
        pl.semaphore_signal(barrier, inc=1, device_id=snd_dev(e), device_id_type=pl.DeviceIdType.MESH)
    for f in range(1, n_m):
        pl.semaphore_signal(barrier, inc=1, device_id=map_dev(f), device_id_type=pl.DeviceIdType.MESH)

    loads = [
        pltpu.make_async_copy(src, dst, local_sem.at[i])
        for i, (src, dst) in enumerate(
            [
                (warm_hbm, warm_in),
                (wet_hbm, wet_in),
                (table_hbm, table),
                (carb_hbm, carb_in),
                (cat_hbm, cat),
                (meas_hbm, mbuf.at[0, 0]),
                (prec_hbm, mbuf.at[0, 1]),
                (q_hbm, q_v),
                (r_hbm, r_v),
                (sens_hbm, sens),
            ]
        )
    ]
    for load in loads:
        load.start()

    row_in = iota((cap, tile), 0)
    for e in range(n_s):
        owner = lax.rem(me + e, n_s)
        whole_id = jnp.full((cap, tile), -1, jnp.int32)
        spot = jnp.full((cap, tile), -1, jnp.int32)
        tile_id = jnp.full((cap, tile), -1, jnp.int32)
        for k in range(cap):
            asked = lists[k, owner]
            t = lax.rem(asked, tiles)
            here = row_in == k
            whole_id = jnp.where(here, jnp.where(asked < 0, -1, owner * (slots * tiles) + asked), whole_id)
            spot = jnp.where(here, t * slots + lax.div(asked, tiles), spot)
            tile_id = jnp.where(here, t, tile_id)
        if e == 0:
            req_recv[0] = spot
        else:
            req_send[e] = spot
        ids[0, pl.ds(e * cap, cap), :] = whole_id
        ids[1, pl.ds(e * cap, cap), :] = tile_id

    pl.semaphore_wait(barrier, n_s - 1 + n_m - 1)

    req = [remote(req_send.at[e], req_recv.at[e], s_req.at[e], r_req.at[e], snd_dev(e)) for e in range(1, n_s)]
    for c in req:
        c.start()
    obs = []
    for f in range(1, n_m):
        obs.append(remote(meas_hbm, mbuf.at[f, 0], s_m.at[f, 0], r_m.at[f, 0], map_dev(f)))
        obs.append(remote(prec_hbm, mbuf.at[f, 1], s_m.at[f, 1], r_m.at[f, 1], map_dev(f)))
    for c in obs:
        c.start()

    carb[...] = jnp.zeros_like(carb)
    for load in loads[:3]:
        load.wait()
    for t in range(tiles):
        lanes = pl.ds(t * tile, tile)
        warm[pl.ds(slots * t, slots), :] = warm_in[:, lanes]
        wet[pl.ds(slots * t, slots), :] = wet_in[:, lanes]
    observed = jnp.concatenate(split3(warm[...]) + split3(wet[...]), axis=1)

    block_row = table[0:1, :]
    block_id = table[2:3, :] * tiles + table[1:2, :]
    asked_hot = onehot(ids[0][:, :nb] == block_id)
    row_hot = onehot(iota((allrows, nb), 0) == block_row)
    tcol[...] = dot(asked_hot, iota((nreq, tile), 0).astype(F32).astype(BF16), ((0,), (0,)))
    rcol[...] = dot(row_hot, iota((allrows, tile), 0).astype(F32).astype(BF16), ((0,), (0,)))

    for c in req:
        c.wait_recv()
    for e in range(n_s):
        ids[0, pl.ds(e * cap, cap), :] = req_recv[e]
    sel = onehot(ids[0] == iota((nreq, tile), 1))
    every = dot(sel, observed, ((1,), (0,)))
    cut = [every[:, i * tile : (i + 1) * tile] for i in range(6)]
    out_warm = (cut[0] + cut[1]) + cut[2]
    out_wet = (cut[3] + cut[4]) + cut[5]
    rep = []
    for e in range(n_s):
        to = rep_recv if e == 0 else rep_send
        to[e, 0:cap, :] = out_warm[e * cap : (e + 1) * cap]
        to[e, cap : 2 * cap, :] = out_wet[e * cap : (e + 1) * cap]
        if e:
            rep.append(remote(rep_send.at[e], rep_recv.at[e], s_rep.at[e], r_rep.at[e], snd_dev(-e)))
            rep[-1].start()
    for load in loads[3:5]:
        load.wait()
    for t in range(tiles):
        carb[pl.ds(4 * t, pools), :] = carb_in[:, pl.ds(t * tile, tile)]
    tile_id = ids[1]
    cls = dot(onehot(tile_id[:, :tiles] == iota((nreq, tiles), 1)), cat[...].astype(F32).astype(BF16), ((1,), (0,)))
    cls = cls.astype(jnp.int32)
    wide = jnp.concatenate([tile_id] * (4 * tiles // tile), axis=1)
    wide_at = iota((nreq, 4 * tiles), 1)
    log_q = jnp.zeros((nreq, tile), F32)
    effects = [jnp.zeros((nreq, tile), F32) for _ in range(pools)]
    for c in range(nclass):
        here = cls == c
        log_q = jnp.where(here, q_s[c], log_q)
        for p in range(pools):
            effects[p] = jnp.where(here, r_s[p, c], effects[p])
    log_q = LOG_BASE_Q + log_q
    held = []
    for p in range(pools):
        carbon = pick(onehot(wide * 4 + p == wide_at), carb[...])
        held.append(RATES[p] * jnp.exp(effects[p]) * carbon)

    for c in rep:
        c.wait_recv()
    for e in range(n_s):
        vecs[0, pl.ds(e * cap, cap), :] = rep_recv[e, 0:cap, :]
        vecs[1, pl.ds(e * cap, cap), :] = rep_recv[e, cap : 2 * cap, :]

    tau = (vecs[0] - BASELINE_CELSIUS) / 10.0
    modifier = jnp.exp(log_q * tau) * vecs[1]
    pieces = [h * modifier for h in held]
    flux = pieces[0] + pieces[1] + pieces[2]
    flux_low = flux.astype(BF16)

    tcol_hot = onehot(tcol[:, :nreq] == iota((nb, nreq), 1).astype(F32))
    vecs_b = dot(tcol_hot, flux_low, ((1,), (0,)))
    model_at = iota((allrows, tile), 0).astype(F32)
    vb[...] = vecs_b
    loads[9].wait()

    def forward(step, acc):
        at = pl.multiple_of(step * CHUNK, CHUNK)
        v = vb[pl.ds(at, CHUNK), :]
        r = rcol[pl.ds(at, CHUNK), :]
        left = [jnp.where(model_at == r[u : u + 1], v[u : u + 1], 0.0).astype(BF16) for u in range(CHUNK)]
        right = [
            sens[pl.ds(pl.multiple_of((step * CHUNK + u) * tile, tile), tile), :] for u in range(CHUNK)
        ]
        return acc + dot(jnp.concatenate(left, axis=1), jnp.concatenate(right, axis=1), ((1,), (1,)))

    part[0] = lax.fori_loop(0, nb // CHUNK, forward, jnp.zeros((allrows, tile), F32))

    swap = [remote(part.at[0], part.at[f], s_p.at[f], r_p.at[f], map_dev(f)) for f in range(1, n_m)]
    for c in swap:
        c.start()
    for c in loads[5:9]:
        c.wait()
    for c in obs:
        c.wait_recv()
    meas, prec = [], []
    for a in range(n_m):
        slot = lax.rem(mm - a + n_m, n_m)
        meas.append(mbuf[slot, 0])
        prec.append(mbuf[slot, 1])
    meas = jnp.concatenate(meas, axis=0)
    prec = jnp.concatenate(prec, axis=0)
    rcol_hot = onehot(rcol[:, :allrows] == iota((nb, allrows), 1).astype(F32))
    for c in swap:
        c.wait_recv()
    total = part[lax.rem(mm + n_m, n_m)]
    for a in range(1, n_m):
        total = total + part[lax.rem(mm - a + n_m, n_m)]
    model[...] = total
    diff = total - meas
    weighted = (diff * prec).astype(BF16)
    own = model[pl.ds(pl.multiple_of(mm * rows, rows), rows), :]
    model_out[...] = own
    outs = [
        pltpu.make_async_copy(src, dst, out_sem.at[i])
        for i, (src, dst) in enumerate(
            [(model_out, model_hbm), (grad_out, grad_hbm), (class_out, class_hbm), (cost_out, cost_hbm)]
        )
    ]
    outs[0].start()
    own_diff = own - mbuf[0, 0]
    misfit = 0.5 * jnp.sum(mbuf[0, 1] * own_diff * own_diff, keepdims=True)

    vb[...] = dot(rcol_hot, weighted, ((1,), (0,)))
    asked_at = iota((nreq, tile), 0).astype(F32)

    def backward(step, acc):
        at = pl.multiple_of(step * CHUNK, CHUNK)
        v = vb[pl.ds(at, CHUNK), :]
        r = tcol[pl.ds(at, CHUNK), :]
        left = [jnp.where(asked_at == r[u : u + 1], v[u : u + 1], 0.0).astype(BF16) for u in range(CHUNK)]
        right = sens[pl.ds(pl.multiple_of(step * CHUNK * tile, CHUNK * tile), CHUNK * tile), :]
        return acc + dot(jnp.concatenate(left, axis=1), right, ((1,), (0,)))

    grads = lax.fori_loop(0, nb // CHUNK, backward, jnp.zeros((nreq, tile), F32))

    terms = [grads * flux * tau] + [grads * piece for piece in pieces]
    for c in range(nclass):
        here = cls == c
        for p, term in enumerate(terms):
            srows[pl.ds(p * nclass + c, 1), :] = jnp.sum(jnp.where(here, term, 0.0), axis=0, keepdims=True)
    sums = jnp.sum(srows[...], axis=1, keepdims=True)
    diagonal = iota((nclass, tile), 0) == iota((nclass, tile), 1)
    lines = []
    for p in range(1 + pools):
        line = jnp.sum(jnp.where(diagonal, sums[p * nclass : (p + 1) * nclass], 0.0), axis=0, keepdims=True)
        if p == 0:
            line = jnp.where(iota((1, tile), 1) == nclass, misfit, line)
        lines.append(line)
    share = jnp.concatenate(lines, axis=0)
    back = []
    for e in range(n_s):
        to = grecv if e == 0 else gsend
        to[e, 0:cap, :] = grads[e * cap : (e + 1) * cap]
        to[e, cap:, :] = share
        if e:
            back.append(remote(gsend.at[e], grecv.at[e], s_g.at[e], r_g.at[e], snd_dev(e)))
            back[-1].start()
    for c in back:
        c.wait_recv()
    share = grecv[0, cap:, :]
    for e in range(1, n_s):
        share = share + grecv[e, cap:, :]
    trecv[0] = share
    last = [remote(trecv.at[0], trecv.at[f], s_t.at[f], r_t.at[f], map_dev(f)) for f in range(1, n_m)]
    for c in last:
        c.start()

    for e in range(n_s):
        vecs[0, pl.ds(e * cap, cap), :] = grecv[e, 0:cap, :]
    hi, mid, low = split3(vecs[0])
    placed = (dot(sel, hi, ((0,), (0,))) + dot(sel, mid, ((0,), (0,)))) + dot(sel, low, ((0,), (0,)))
    fg[...] = placed
    for t in range(tiles):
        grad_out[:, pl.ds(t * tile, tile)] = fg[pl.ds(slots * t, slots), :]
    outs[1].start()

    for c in last:
        c.wait_recv()
    share = trecv[lax.rem(mm + n_m, n_m)]
    for a in range(1, n_m):
        share = share + trecv[lax.rem(mm - a + n_m, n_m)]
    class_out[0:1, :] = share[0:1, :nclass] + q_v[...] / PRIOR_VAR
    class_out[1:, :] = share[1:, :nclass] + r_v[...] / PRIOR_VAR
    prior = jnp.sum(q_v[...] * q_v[...], keepdims=True) + jnp.sum(r_v[...] * r_v[...], keepdims=True)
    cost_out[...] = share[0:1, nclass : nclass + 1] + 0.5 * prior / PRIOR_VAR

    outs[2].start()
    outs[3].start()
    for c in req + obs + rep + swap + back + last:
        c.wait_send()
    for c in outs:
        c.wait()


def hand_over(*refs):
    n = len(refs) // 2
    copies = [pltpu.make_async_copy(refs[i], refs[n + i], refs[2 * n].at[i]) for i in range(n)]
    for c in copies:
        c.start()
    for c in copies:
        c.wait()


def shards(
    n_s,
    n_m,
    sensitivity_blocks,
    block_placement_table,
    needed_tile_lists,
    location_category,
    ground_warmth_celsius,
    wetness_factor,
    carbon_reservoirs,
    category_sensitivity_effect,
    reservoir_decay_effect,
    measured_anomaly,
    retrieval_precision,
):
    nb, tile, _ = sensitivity_blocks.shape
    slots, cells = ground_warmth_celsius.shape
    pools, nclass = reservoir_decay_effect.shape
    tiles = cells // tile
    cap = needed_tile_lists.shape[1]
    nreq = n_s * cap
    rows = measured_anomaly.shape[0]
    allrows = rows * n_m
    hbm = pl.BlockSpec(memory_space=pl.ANY)
    results = (
        jax.ShapeDtypeStruct((rows, tile), F32),
        jax.ShapeDtypeStruct((slots, cells), F32),
        jax.ShapeDtypeStruct((1 + pools, nclass), F32),
        jax.ShapeDtypeStruct((1, 1), F32),
    )
    smem = pl.BlockSpec(memory_space=pltpu.SMEM)
    sem = pltpu.SemaphoreType.DMA
    blocks = nb * tile
    outs = pl.pallas_call(
        functools.partial(kernel, n_s, n_m),
        out_shape=results,
        in_specs=[hbm, hbm, smem, hbm, hbm, hbm, hbm, smem, smem, hbm, hbm, hbm, hbm],
        out_specs=(hbm,) * 4,
        scratch_shapes=[
            pltpu.VMEM((rows, tile), F32),
            pltpu.VMEM((slots, cells), F32),
            pltpu.VMEM((1 + pools, nclass), F32),
            pltpu.VMEM((1, 1), F32),
            pltpu.VMEM((3, nb), jnp.int32),
            pltpu.VMEM((1, nclass), F32),
            pltpu.VMEM((pools, nclass), F32),
            pltpu.VMEM((nb, tile), F32),
            pltpu.VMEM((blocks, tile), BF16),
            pltpu.VMEM((tiles, tile), jnp.int32),
            pltpu.VMEM((slots, cells), F32),
            pltpu.VMEM((slots, cells), F32),
            pltpu.VMEM((pools, cells), F32),
            pltpu.VMEM((tiles * slots, tile), F32),
            pltpu.VMEM((tiles * slots, tile), F32),
            pltpu.VMEM((tiles * 4, tile), F32),
            pltpu.VMEM((n_s, cap, tile), jnp.int32),
            pltpu.VMEM((n_s, cap, tile), jnp.int32),
            pltpu.VMEM((n_s, 2 * cap, tile), F32),
            pltpu.VMEM((n_s, 2 * cap, tile), F32),
            pltpu.VMEM((n_m, 2, rows, tile), F32),
            pltpu.VMEM((n_m, allrows, tile), F32),
            pltpu.VMEM((n_s, cap + 1 + pools, tile), F32),
            pltpu.VMEM((n_s, cap + 1 + pools, tile), F32),
            pltpu.VMEM((1 + pools, tile), F32),
            pltpu.VMEM((n_m, 1 + pools, tile), F32),
            pltpu.VMEM((2, nreq, tile), jnp.int32),
            pltpu.VMEM((2, nreq, tile), F32),
            pltpu.VMEM((nb, tile), F32),
            pltpu.VMEM((nb, tile), F32),
            pltpu.VMEM((allrows, tile), F32),
            pltpu.VMEM((tiles * slots, tile), F32),
            pltpu.VMEM(((1 + pools) * nclass, tile), F32),
            sem((10,)),
            sem((4,)),
            sem((n_s,)),
            sem((n_s,)),
            sem((n_s,)),
            sem((n_s,)),
            sem((n_m, 2)),
            sem((n_m, 2)),
            sem((n_m,)),
            sem((n_m,)),
            sem((n_s,)),
            sem((n_s,)),
            sem((n_m,)),
            sem((n_m,)),
        ],
        compiler_params=pltpu.CompilerParams(collective_id=0, has_side_effects=True),
        cost_estimate=pl.CostEstimate(
            flops=2 * blocks * tile * (allrows + nreq), bytes_accessed=2 * blocks * tile, transcendentals=4 * nreq * tile
        ),
        name="inversion",
    )(
        sensitivity_blocks.reshape(blocks, tile),
        block_placement_table,
        needed_tile_lists.T,
        location_category.reshape(tiles, tile),
        ground_warmth_celsius,
        wetness_factor,
        carbon_reservoirs,
        category_sensitivity_effect,
        reservoir_decay_effect,
        category_sensitivity_effect.reshape(1, nclass),
        reservoir_decay_effect,
        measured_anomaly,
        retrieval_precision,
    )
    model, grad, classes, cost = pl.pallas_call(
        hand_over,
        out_shape=results,
        in_specs=[hbm] * 4,
        out_specs=(hbm,) * 4,
        scratch_shapes=[sem((4,))],
        name="results",
    )(*outs)
    return model, grad, classes, cost.reshape(())


def solution(mesh):
    in_specs = (
        P(("snd", "map"), None, None),
        P(None, ("snd", "map")),
        P(("snd", "map"), None),
        P("map"),
        P("snd", "map"),
        P("snd", "map"),
        P(None, "map"),
        P(),
        P(),
        P(("snd", "map"), None),
        P(("snd", "map"), None),
    )
    out_specs = (P(("snd", "map"), None), P("snd", "map"), P(), P())
    return jax.shard_map(
        functools.partial(shards, mesh.shape["snd"], mesh.shape["map"]),
        mesh=mesh,
        in_specs=in_specs,
        out_specs=out_specs,
        check_vma=False,
    )
```

```python
import functools

import jax
import jax.numpy as jnp
from jax import lax
from jax.experimental import pallas as pl
from jax.experimental.pallas import tpu as pltpu
from jax.sharding import PartitionSpec as P

BASELINE_CELSIUS = 15.0
LOG_BASE_Q = 0.6931471805599453
PRIOR_VAR = 0.09
RATES = (0.6, 0.25, 0.1)
CHUNK = 16
F32 = jnp.float32
BF16 = jnp.bfloat16


def split3(x):
    hi = x.astype(BF16)
    rest = x - hi.astype(F32)
    mid = rest.astype(BF16)
    low = (rest - mid.astype(F32)).astype(BF16)
    return hi, mid, low


def dot(a, b, dims):
    return lax.dot_general(a, b, (dims, ((), ())), preferred_element_type=F32)


def onehot(mask):
    return jnp.where(mask, 1.0, 0.0).astype(BF16)


def pick(sel, x):
    hi, mid, low = split3(x)
    return (dot(sel, hi, ((1,), (0,))) + dot(sel, mid, ((1,), (0,)))) + dot(sel, low, ((1,), (0,)))


def iota(shape, dim):
    return lax.broadcasted_iota(jnp.int32, shape, dim)


def kernel(
    n_s, n_m, sens_hbm, table_hbm, lists, cat_hbm, warm_hbm, wet_hbm, carb_hbm, q_s, r_s, q_hbm, r_hbm, meas_hbm,
    prec_hbm, model_hbm, grad_hbm, class_hbm, cost_hbm,
    model_out, grad_out, class_out, cost_out, table, q_v, r_v, vb, sens, cat, warm_in, wet_in, carb_in, warm, wet, carb,
    req_send, req_recv, rep_send, rep_recv, mbuf, part, gsend, grecv, tsend, trecv,
    ids, vecs, tcol, rcol, model, fg, srows,
    local_sem, out_sem, s_req, r_req, s_rep, r_rep, s_m, r_m, s_p, r_p, s_g, r_g, s_t, r_t,
):
    cap = lists.shape[0]
    nreq = n_s * cap
    slots = warm_hbm.shape[0]
    tiles = cat.shape[0]
    nclass = q_s.shape[0]
    pools = carb_hbm.shape[0]
    rows = meas_hbm.shape[0]
    allrows = rows * n_m
    nb = table.shape[1]
    tile = sens.shape[1]
    me = lax.axis_index("snd")
    mm = lax.axis_index("map")
    snd_dev = lambda e: {"snd": lax.rem(me + e + n_s, n_s)}
    map_dev = lambda f: {"map": lax.rem(mm + f + n_m, n_m)}

    def remote(src, dst, ss, rs, dev):
        return pltpu.make_async_remote_copy(
            src_ref=src, dst_ref=dst, send_sem=ss, recv_sem=rs, device_id=dev, device_id_type=pl.DeviceIdType.MESH
        )

    barrier = pltpu.get_barrier_semaphore()
    for e in range(1, n_s):
        pl.semaphore_signal(barrier, inc=1, device_id=snd_dev(e), device_id_type=pl.DeviceIdType.MESH)
    for f in range(1, n_m):
        pl.semaphore_signal(barrier, inc=1, device_id=map_dev(f), device_id_type=pl.DeviceIdType.MESH)

    loads = [
        pltpu.make_async_copy(src, dst, local_sem.at[i])
        for i, (src, dst) in enumerate(
            [
                (warm_hbm, warm_in),
                (wet_hbm, wet_in),
                (table_hbm, table),
                (carb_hbm, carb_in),
                (cat_hbm, cat),
                (meas_hbm, mbuf.at[0, 0]),
                (prec_hbm, mbuf.at[0, 1]),
                (q_hbm, q_v),
                (r_hbm, r_v),
                (sens_hbm, sens),
            ]
        )
    ]
    for load in loads:
        load.start()

    row_in = iota((cap, tile), 0)
    for e in range(n_s):
        owner = lax.rem(me + e, n_s)
        whole_id = jnp.full((cap, tile), -1, jnp.int32)
        spot = jnp.full((cap, tile), -1, jnp.int32)
        tile_id = jnp.full((cap, tile), -1, jnp.int32)
        for k in range(cap):
            asked = lists[k, owner]
            t = lax.rem(asked, tiles)
            here = row_in == k
            whole_id = jnp.where(here, jnp.where(asked < 0, -1, owner * (slots * tiles) + asked), whole_id)
            spot = jnp.where(here, t * slots + lax.div(asked, tiles), spot)
            tile_id = jnp.where(here, t, tile_id)
        if e == 0:
            req_recv[0] = spot
        else:
            req_send[e] = spot
        ids[0, pl.ds(e * cap, cap), :] = whole_id
        ids[1, pl.ds(e * cap, cap), :] = tile_id

    pl.semaphore_wait(barrier, n_s - 1 + n_m - 1)

    req = [remote(req_send.at[e], req_recv.at[e], s_req.at[e], r_req.at[e], snd_dev(e)) for e in range(1, n_s)]
    for c in req:
        c.start()
    obs = []
    for f in range(1, n_m):
        obs.append(remote(meas_hbm, mbuf.at[f, 0], s_m.at[f, 0], r_m.at[f, 0], map_dev(f)))
        obs.append(remote(prec_hbm, mbuf.at[f, 1], s_m.at[f, 1], r_m.at[f, 1], map_dev(f)))
    for c in obs:
        c.start()

    carb[...] = jnp.zeros_like(carb)
    for load in loads[:3]:
        load.wait()
    for t in range(tiles):
        lanes = pl.ds(t * tile, tile)
        warm[pl.ds(slots * t, slots), :] = warm_in[:, lanes]
        wet[pl.ds(slots * t, slots), :] = wet_in[:, lanes]
    observed = jnp.concatenate(split3(warm[...]) + split3(wet[...]), axis=1)

    block_row = table[0:1, :]
    block_id = table[2:3, :] * tiles + table[1:2, :]
    asked_hot = onehot(ids[0][:, :nb] == block_id)
    row_hot = onehot(iota((allrows, nb), 0) == block_row)
    tcol[...] = dot(asked_hot, iota((nreq, tile), 0).astype(F32).astype(BF16), ((0,), (0,)))
    rcol[...] = dot(row_hot, iota((allrows, tile), 0).astype(F32).astype(BF16), ((0,), (0,)))

    for c in req:
        c.wait_recv()
    for e in range(n_s):
        ids[0, pl.ds(e * cap, cap), :] = req_recv[e]
    sel = onehot(ids[0] == iota((nreq, tile), 1))
    every = dot(sel, observed, ((1,), (0,)))
    cut = [every[:, i * tile : (i + 1) * tile] for i in range(6)]
    out_warm = (cut[0] + cut[1]) + cut[2]
    out_wet = (cut[3] + cut[4]) + cut[5]
    rep = []
    for e in range(n_s):
        to = rep_recv if e == 0 else rep_send
        to[e, 0:cap, :] = out_warm[e * cap : (e + 1) * cap]
        to[e, cap : 2 * cap, :] = out_wet[e * cap : (e + 1) * cap]
        if e:
            rep.append(remote(rep_send.at[e], rep_recv.at[e], s_rep.at[e], r_rep.at[e], snd_dev(-e)))
            rep[-1].start()
    for load in loads[3:5]:
        load.wait()
    for t in range(tiles):
        carb[pl.ds(4 * t, pools), :] = carb_in[:, pl.ds(t * tile, tile)]
    tile_id = ids[1]
    cls = dot(onehot(tile_id[:, :tiles] == iota((nreq, tiles), 1)), cat[...].astype(F32).astype(BF16), ((1,), (0,)))
    cls = cls.astype(jnp.int32)
    wide = jnp.concatenate([tile_id] * (4 * tiles // tile), axis=1)
    wide_at = iota((nreq, 4 * tiles), 1)
    log_q = jnp.zeros((nreq, tile), F32)
    effects = [jnp.zeros((nreq, tile), F32) for _ in range(pools)]
    for c in range(nclass):
        here = cls == c
        log_q = jnp.where(here, q_s[c], log_q)
        for p in range(pools):
            effects[p] = jnp.where(here, r_s[p, c], effects[p])
    log_q = LOG_BASE_Q + log_q
    held = []
    for p in range(pools):
        carbon = pick(onehot(wide * 4 + p == wide_at), carb[...])
        held.append(RATES[p] * jnp.exp(effects[p]) * carbon)

    tcol_hot = onehot(tcol[:, :nreq] == iota((nb, nreq), 1).astype(F32))
    for c in rep:
        c.wait_recv()
    for e in range(n_s):
        vecs[0, pl.ds(e * cap, cap), :] = rep_recv[e, 0:cap, :]
        vecs[1, pl.ds(e * cap, cap), :] = rep_recv[e, cap : 2 * cap, :]

    tau = (vecs[0] - BASELINE_CELSIUS) / 10.0
    modifier = jnp.exp(log_q * tau) * vecs[1]
    pieces = [h * modifier for h in held]
    flux = pieces[0] + pieces[1] + pieces[2]
    flux_low = flux.astype(BF16)

    vecs_b = dot(tcol_hot, flux_low, ((1,), (0,)))
    model_at = iota((allrows, tile), 0).astype(F32)
    vb[...] = vecs_b
    loads[9].wait()

    partial = jnp.zeros((allrows, tile), F32)
    for at in range(0, nb, CHUNK):
        left = [
            jnp.where(model_at == rcol[b : b + 1, :], vb[b : b + 1, :], 0.0).astype(BF16) for b in range(at, at + CHUNK)
        ]
        right = [sens[b * tile : (b + 1) * tile, :] for b in range(at, at + CHUNK)]
        partial += dot(jnp.concatenate(left, axis=1), jnp.concatenate(right, axis=1), ((1,), (1,)))
    part[0] = partial

    swap = [remote(part.at[0], part.at[f], s_p.at[f], r_p.at[f], map_dev(f)) for f in range(1, n_m)]
    for c in swap:
        c.start()
    for c in loads[5:9]:
        c.wait()
    for c in obs:
        c.wait_recv()
    meas, prec = [], []
    for a in range(n_m):
        slot = lax.rem(mm - a + n_m, n_m)
        meas.append(mbuf[slot, 0])
        prec.append(mbuf[slot, 1])
    meas = jnp.concatenate(meas, axis=0)
    prec = jnp.concatenate(prec, axis=0)
    rcol_hot = onehot(rcol[:, :allrows] == iota((nb, allrows), 1).astype(F32))
    for c in swap:
        c.wait_recv()
    total = part[lax.rem(mm + n_m, n_m)]
    for a in range(1, n_m):
        total = total + part[lax.rem(mm - a + n_m, n_m)]
    model[...] = total
    diff = total - meas
    weighted = (diff * prec).astype(BF16)
    own = model[pl.ds(pl.multiple_of(mm * rows, rows), rows), :]
    model_out[...] = own
    outs = [
        pltpu.make_async_copy(src, dst, out_sem.at[i])
        for i, (src, dst) in enumerate(
            [(model_out, model_hbm), (grad_out, grad_hbm), (class_out, class_hbm), (cost_out, cost_hbm)]
        )
    ]
    outs[0].start()
    own_diff = own - mbuf[0, 0]
    misfit = 0.5 * jnp.sum(mbuf[0, 1] * own_diff * own_diff, keepdims=True)

    vb[...] = dot(rcol_hot, weighted, ((1,), (0,)))
    asked_at = iota((nreq, tile), 0).astype(F32)

    grads = jnp.zeros((nreq, tile), F32)
    for at in range(0, nb, CHUNK):
        left = [
            jnp.where(asked_at == tcol[b : b + 1, :], vb[b : b + 1, :], 0.0).astype(BF16) for b in range(at, at + CHUNK)
        ]
        grads += dot(jnp.concatenate(left, axis=1), sens[at * tile : (at + CHUNK) * tile, :], ((1,), (0,)))

    terms = [grads * flux * tau] + [grads * piece for piece in pieces]
    for c in range(nclass):
        here = cls == c
        for p, term in enumerate(terms):
            srows[pl.ds(p * nclass + c, 1), :] = jnp.sum(jnp.where(here, term, 0.0), axis=0, keepdims=True)
    sums = jnp.sum(srows[...], axis=1, keepdims=True)
    diagonal = iota((nclass, tile), 0) == iota((nclass, tile), 1)
    lines = []
    for p in range(1 + pools):
        line = jnp.sum(jnp.where(diagonal, sums[p * nclass : (p + 1) * nclass], 0.0), axis=0, keepdims=True)
        if p == 0:
            line = jnp.where(iota((1, tile), 1) == nclass, misfit, line)
        lines.append(line)
    share = jnp.concatenate(lines, axis=0)
    back = []
    for e in range(n_s):
        to = grecv if e == 0 else gsend
        to[e, 0:cap, :] = grads[e * cap : (e + 1) * cap]
        to[e, cap:, :] = share
        if e:
            back.append(remote(gsend.at[e], grecv.at[e], s_g.at[e], r_g.at[e], snd_dev(e)))
            back[-1].start()
    for c in back:
        c.wait_recv()
    share = grecv[0, cap:, :]
    for e in range(1, n_s):
        share = share + grecv[e, cap:, :]
    trecv[0] = share
    last = [remote(trecv.at[0], trecv.at[f], s_t.at[f], r_t.at[f], map_dev(f)) for f in range(1, n_m)]
    for c in last:
        c.start()

    for e in range(n_s):
        vecs[0, pl.ds(e * cap, cap), :] = grecv[e, 0:cap, :]
    hi, mid, low = split3(vecs[0])
    placed = (dot(sel, hi, ((0,), (0,))) + dot(sel, mid, ((0,), (0,)))) + dot(sel, low, ((0,), (0,)))
    fg[...] = placed
    for t in range(tiles):
        grad_out[:, pl.ds(t * tile, tile)] = fg[pl.ds(slots * t, slots), :]
    outs[1].start()

    for c in last:
        c.wait_recv()
    share = trecv[lax.rem(mm + n_m, n_m)]
    for a in range(1, n_m):
        share = share + trecv[lax.rem(mm - a + n_m, n_m)]
    class_out[0:1, :] = share[0:1, :nclass] + q_v[...] / PRIOR_VAR
    class_out[1:, :] = share[1:, :nclass] + r_v[...] / PRIOR_VAR
    prior = jnp.sum(q_v[...] * q_v[...], keepdims=True) + jnp.sum(r_v[...] * r_v[...], keepdims=True)
    cost_out[...] = share[0:1, nclass : nclass + 1] + 0.5 * prior / PRIOR_VAR

    outs[2].start()
    outs[3].start()
    for c in req + obs + rep + swap + back + last:
        c.wait_send()
    for c in outs:
        c.wait()


def hand_over(*refs):
    n = len(refs) // 3
    given, results, held, (sem_in, sem_out) = refs[:n], refs[n : 2 * n], refs[2 * n : 3 * n], refs[3 * n :]
    fetch = [pltpu.make_async_copy(given[i], held[i], sem_in.at[i]) for i in range(n)]
    write = [pltpu.make_async_copy(held[i], results[i], sem_out.at[i]) for i in range(n)]
    for c in fetch:
        c.start()
    for c, w in zip(fetch, write):
        c.wait()
        w.start()
    for w in write:
        w.wait()


def shards(
    n_s,
    n_m,
    sensitivity_blocks,
    block_placement_table,
    needed_tile_lists,
    location_category,
    ground_warmth_celsius,
    wetness_factor,
    carbon_reservoirs,
    category_sensitivity_effect,
    reservoir_decay_effect,
    measured_anomaly,
    retrieval_precision,
):
    nb, tile, _ = sensitivity_blocks.shape
    slots, cells = ground_warmth_celsius.shape
    pools, nclass = reservoir_decay_effect.shape
    tiles = cells // tile
    cap = needed_tile_lists.shape[1]
    nreq = n_s * cap
    rows = measured_anomaly.shape[0]
    allrows = rows * n_m
    hbm = pl.BlockSpec(memory_space=pl.ANY)
    results = (
        jax.ShapeDtypeStruct((rows, tile), F32),
        jax.ShapeDtypeStruct((slots, cells), F32),
        jax.ShapeDtypeStruct((1 + pools, nclass), F32),
        jax.ShapeDtypeStruct((1, 1), F32),
    )
    smem = pl.BlockSpec(memory_space=pltpu.SMEM)
    sem = pltpu.SemaphoreType.DMA
    blocks = nb * tile
    outs = pl.pallas_call(
        functools.partial(kernel, n_s, n_m),
        out_shape=results,
        in_specs=[hbm, hbm, smem, hbm, hbm, hbm, hbm, smem, smem, hbm, hbm, hbm, hbm],
        out_specs=(hbm,) * 4,
        scratch_shapes=[
            pltpu.VMEM((rows, tile), F32),
            pltpu.VMEM((slots, cells), F32),
            pltpu.VMEM((1 + pools, nclass), F32),
            pltpu.VMEM((1, 1), F32),
            pltpu.VMEM((3, nb), jnp.int32),
            pltpu.VMEM((1, nclass), F32),
            pltpu.VMEM((pools, nclass), F32),
            pltpu.VMEM((nb, tile), F32),
            pltpu.VMEM((blocks, tile), BF16),
            pltpu.VMEM((tiles, tile), jnp.int32),
            pltpu.VMEM((slots, cells), F32),
            pltpu.VMEM((slots, cells), F32),
            pltpu.VMEM((pools, cells), F32),
            pltpu.VMEM((tiles * slots, tile), F32),
            pltpu.VMEM((tiles * slots, tile), F32),
            pltpu.VMEM((tiles * 4, tile), F32),
            pltpu.VMEM((n_s, cap, tile), jnp.int32),
            pltpu.VMEM((n_s, cap, tile), jnp.int32),
            pltpu.VMEM((n_s, 2 * cap, tile), F32),
            pltpu.VMEM((n_s, 2 * cap, tile), F32),
            pltpu.VMEM((n_m, 2, rows, tile), F32),
            pltpu.VMEM((n_m, allrows, tile), F32),
            pltpu.VMEM((n_s, cap + 1 + pools, tile), F32),
            pltpu.VMEM((n_s, cap + 1 + pools, tile), F32),
            pltpu.VMEM((1 + pools, tile), F32),
            pltpu.VMEM((n_m, 1 + pools, tile), F32),
            pltpu.VMEM((2, nreq, tile), jnp.int32),
            pltpu.VMEM((2, nreq, tile), F32),
            pltpu.VMEM((nb, tile), F32),
            pltpu.VMEM((nb, tile), F32),
            pltpu.VMEM((allrows, tile), F32),
            pltpu.VMEM((tiles * slots, tile), F32),
            pltpu.VMEM(((1 + pools) * nclass, tile), F32),
            sem((10,)),
            sem((4,)),
            sem((n_s,)),
            sem((n_s,)),
            sem((n_s,)),
            sem((n_s,)),
            sem((n_m, 2)),
            sem((n_m, 2)),
            sem((n_m,)),
            sem((n_m,)),
            sem((n_s,)),
            sem((n_s,)),
            sem((n_m,)),
            sem((n_m,)),
        ],
        compiler_params=pltpu.CompilerParams(collective_id=0, has_side_effects=True),
        cost_estimate=pl.CostEstimate(
            flops=2 * blocks * tile * (allrows + nreq), bytes_accessed=2 * blocks * tile, transcendentals=4 * nreq * tile
        ),
        name="inversion",
    )(
        sensitivity_blocks.reshape(blocks, tile),
        block_placement_table,
        needed_tile_lists.T,
        location_category.reshape(tiles, tile),
        ground_warmth_celsius,
        wetness_factor,
        carbon_reservoirs,
        category_sensitivity_effect,
        reservoir_decay_effect,
        category_sensitivity_effect.reshape(1, nclass),
        reservoir_decay_effect,
        measured_anomaly,
        retrieval_precision,
    )
    model, grad, classes, cost = pl.pallas_call(
        hand_over,
        out_shape=results,
        in_specs=[hbm] * 4,
        out_specs=(hbm,) * 4,
        scratch_shapes=[pltpu.VMEM(r.shape, F32) for r in results] + [sem((4,)), sem((4,))],
        name="results",
    )(*outs)
    return model, grad, classes, cost.reshape(())


def solution(mesh):
    in_specs = (
        P(("snd", "map"), None, None),
        P(None, ("snd", "map")),
        P(("snd", "map"), None),
        P("map"),
        P("snd", "map"),
        P("snd", "map"),
        P(None, "map"),
        P(),
        P(),
        P(("snd", "map"), None),
        P(("snd", "map"), None),
    )
    out_specs = (P(("snd", "map"), None), P("snd", "map"), P(), P())
    return jax.shard_map(
        functools.partial(shards, mesh.shape["snd"], mesh.shape["map"]),
        mesh=mesh,
        in_specs=in_specs,
        out_specs=out_specs,
        check_vma=False,
    )
```

```python
import functools

import jax
import jax.numpy as jnp
from jax import lax
from jax.experimental import pallas as pl
from jax.experimental.pallas import tpu as pltpu
from jax.sharding import PartitionSpec as P

BASELINE_CELSIUS = 15.0
LOG_BASE_Q = 0.6931471805599453
PRIOR_VAR = 0.09
RATES = (0.6, 0.25, 0.1)
CHUNK = 16
F32 = jnp.float32
BF16 = jnp.bfloat16


def split3(x):
    hi = x.astype(BF16)
    rest = x - hi.astype(F32)
    mid = rest.astype(BF16)
    low = (rest - mid.astype(F32)).astype(BF16)
    return hi, mid, low


def dot(a, b, dims):
    return lax.dot_general(a, b, (dims, ((), ())), preferred_element_type=F32)


def onehot(mask):
    return jnp.where(mask, 1.0, 0.0).astype(BF16)


def pick(sel, x):
    hi, mid, low = split3(x)
    return (dot(sel, hi, ((1,), (0,))) + dot(sel, mid, ((1,), (0,)))) + dot(sel, low, ((1,), (0,)))


def iota(shape, dim):
    return lax.broadcasted_iota(jnp.int32, shape, dim)


def is_direct(n_s, n_m):
    return n_s * n_m <= 64


def kernel(
    n_s, n_m, sens_hbm, table_hbm, lists, cat_hbm, warm_hbm, wet_hbm, carb_hbm, q_s, r_s, q_hbm, r_hbm, meas_hbm,
    prec_hbm,
    model_out, grad_out, class_out, cost_out, table, q_v, r_v, vb, sens, cat, warm_in, wet_in, carb_in, warm, wet, carb,
    req_send, req_recv, rep_send, rep_recv, mbuf, part, gsend, grecv, tsend, trecv,
    ids, vecs, tcol, rcol, model, fg, srows,
    local_sem, s_req, r_req, s_rep, r_rep, s_m, r_m, s_p, r_p, s_g, r_g, s_t, r_t,
):
    cap = lists.shape[0]
    nreq = n_s * cap
    slots = warm_hbm.shape[0]
    tiles = cat.shape[0]
    nclass = q_s.shape[0]
    pools = carb_hbm.shape[0]
    rows = meas_hbm.shape[0]
    allrows = rows * n_m
    nb = table.shape[1]
    tile = sens.shape[1]
    me = lax.axis_index("snd")
    mm = lax.axis_index("map")
    snd_dev = lambda e: {"snd": lax.rem(me + e + n_s, n_s)}
    map_dev = lambda f: {"map": lax.rem(mm + f + n_m, n_m)}

    def remote(src, dst, ss, rs, dev):
        return pltpu.make_async_remote_copy(
            src_ref=src, dst_ref=dst, send_sem=ss, recv_sem=rs, device_id=dev, device_id_type=pl.DeviceIdType.MESH
        )

    barrier = pltpu.get_barrier_semaphore()
    direct = is_direct(n_s, n_m)
    others = [(e, f) for e in range(n_s) for f in range(n_m) if e + f and (direct or e == 0 or f == 0)]
    for e, f in others:
        pl.semaphore_signal(barrier, inc=1, device_id=snd_dev(e) | map_dev(f), device_id_type=pl.DeviceIdType.MESH)

    loads = [
        pltpu.make_async_copy(src, dst, local_sem.at[i])
        for i, (src, dst) in enumerate(
            [
                (warm_hbm, warm_in),
                (wet_hbm, wet_in),
                (table_hbm, table),
                (carb_hbm, carb_in),
                (cat_hbm, cat),
                (meas_hbm, mbuf.at[0, 0]),
                (prec_hbm, mbuf.at[0, 1]),
                (q_hbm, q_v),
                (r_hbm, r_v),
                (sens_hbm, sens),
            ]
        )
    ]
    for load in loads:
        load.start()

    row_in = iota((cap, tile), 0)
    for e in range(n_s):
        owner = lax.rem(me + e, n_s)
        whole_id = jnp.full((cap, tile), -1, jnp.int32)
        spot = jnp.full((cap, tile), -1, jnp.int32)
        tile_id = jnp.full((cap, tile), -1, jnp.int32)
        for k in range(cap):
            asked = lists[k, owner]
            t = lax.rem(asked, tiles)
            here = row_in == k
            whole_id = jnp.where(here, jnp.where(asked < 0, -1, owner * (slots * tiles) + asked), whole_id)
            spot = jnp.where(here, t * slots + lax.div(asked, tiles), spot)
            tile_id = jnp.where(here, t, tile_id)
        if e == 0:
            req_recv[0] = spot
        else:
            req_send[e] = spot
        ids[0, pl.ds(e * cap, cap), :] = whole_id
        ids[1, pl.ds(e * cap, cap), :] = tile_id

    pl.semaphore_wait(barrier, len(others))

    req = [remote(req_send.at[e], req_recv.at[e], s_req.at[e], r_req.at[e], snd_dev(e)) for e in range(1, n_s)]
    for c in req:
        c.start()
    carb[...] = jnp.zeros_like(carb)
    for load in loads[:3]:
        load.wait()
    for t in range(tiles):
        lanes = pl.ds(t * tile, tile)
        warm[pl.ds(slots * t, slots), :] = warm_in[:, lanes]
        wet[pl.ds(slots * t, slots), :] = wet_in[:, lanes]
    observed = jnp.concatenate(split3(warm[...]) + split3(wet[...]), axis=1)

    block_row = table[0:1, :]
    block_id = table[2:3, :] * tiles + table[1:2, :]
    asked_hot = onehot(ids[0][:, :nb] == block_id)
    row_hot = onehot(iota((allrows, nb), 0) == block_row)
    tcol[...] = dot(asked_hot, iota((nreq, tile), 0).astype(F32).astype(BF16), ((0,), (0,)))
    rcol[...] = dot(row_hot, iota((allrows, tile), 0).astype(F32).astype(BF16), ((0,), (0,)))

    for c in req:
        c.wait_recv()
    for e in range(n_s):
        ids[0, pl.ds(e * cap, cap), :] = req_recv[e]
    sel = onehot(ids[0] == iota((nreq, tile), 1))
    every = dot(sel, observed, ((1,), (0,)))
    cut = [every[:, i * tile : (i + 1) * tile] for i in range(6)]
    out_warm = (cut[0] + cut[1]) + cut[2]
    out_wet = (cut[3] + cut[4]) + cut[5]
    rep = []
    for e in range(n_s):
        to = rep_recv if e == 0 else rep_send
        to[e, 0:cap, :] = out_warm[e * cap : (e + 1) * cap]
        to[e, cap : 2 * cap, :] = out_wet[e * cap : (e + 1) * cap]
        if e:
            rep.append(remote(rep_send.at[e], rep_recv.at[e], s_rep.at[e], r_rep.at[e], snd_dev(-e)))
            rep[-1].start()
    for load in loads[5:7]:
        load.wait()
    obs = [remote(mbuf.at[0], mbuf.at[f], s_m.at[f], r_m.at[f], map_dev(f)) for f in range(1, n_m)]
    for c in obs:
        c.start()

    for load in loads[3:5]:
        load.wait()
    for t in range(tiles):
        carb[pl.ds(4 * t, pools), :] = carb_in[:, pl.ds(t * tile, tile)]
    tile_id = ids[1]
    cls = dot(onehot(tile_id[:, :tiles] == iota((nreq, tiles), 1)), cat[...].astype(F32).astype(BF16), ((1,), (0,)))
    cls = cls.astype(jnp.int32)
    wide = jnp.concatenate([tile_id] * (4 * tiles // tile), axis=1)
    wide_at = iota((nreq, 4 * tiles), 1)
    log_q = jnp.zeros((nreq, tile), F32)
    effects = [jnp.zeros((nreq, tile), F32) for _ in range(pools)]
    for c in range(nclass):
        here = cls == c
        log_q = jnp.where(here, q_s[c], log_q)
        for p in range(pools):
            effects[p] = jnp.where(here, r_s[p, c], effects[p])
    log_q = LOG_BASE_Q + log_q
    held = []
    for p in range(pools):
        carbon = pick(onehot(wide * 4 + p == wide_at), carb[...])
        held.append(RATES[p] * jnp.exp(effects[p]) * carbon)

    tcol_hot = onehot(tcol[:, :nreq] == iota((nb, nreq), 1).astype(F32))
    for c in rep:
        c.wait_recv()
    for e in range(n_s):
        vecs[0, pl.ds(e * cap, cap), :] = rep_recv[e, 0:cap, :]
        vecs[1, pl.ds(e * cap, cap), :] = rep_recv[e, cap : 2 * cap, :]

    tau = (vecs[0] - BASELINE_CELSIUS) / 10.0
    modifier = jnp.exp(log_q * tau) * vecs[1]
    pieces = [h * modifier for h in held]
    flux = pieces[0] + pieces[1] + pieces[2]
    flux_low = flux.astype(BF16)

    vecs_b = dot(tcol_hot, flux_low, ((1,), (0,)))
    model_at = iota((allrows, tile), 0).astype(F32)
    vb[...] = vecs_b
    loads[9].wait()

    partial = jnp.zeros((allrows, tile), F32)
    for at in range(0, nb, CHUNK):
        left = [
            jnp.where(model_at == rcol[b : b + 1, :], vb[b : b + 1, :], 0.0).astype(BF16) for b in range(at, at + CHUNK)
        ]
        right = [sens[b * tile : (b + 1) * tile, :] for b in range(at, at + CHUNK)]
        partial += dot(jnp.concatenate(left, axis=1), jnp.concatenate(right, axis=1), ((1,), (1,)))
    part[0] = partial

    swap = [remote(part.at[0], part.at[f], s_p.at[f], r_p.at[f], map_dev(f)) for f in range(1, n_m)]
    for c in swap:
        c.start()
    for c in loads[7:9]:
        c.wait()
    for c in obs:
        c.wait_recv()
    meas, prec = [], []
    for a in range(n_m):
        slot = lax.rem(mm - a + n_m, n_m)
        meas.append(mbuf[slot, 0])
        prec.append(mbuf[slot, 1])
    meas = jnp.concatenate(meas, axis=0)
    prec = jnp.concatenate(prec, axis=0)
    rcol_hot = onehot(rcol[:, :allrows] == iota((nb, allrows), 1).astype(F32))
    for c in swap:
        c.wait_recv()
    total = part[lax.rem(mm + n_m, n_m)]
    for a in range(1, n_m):
        total = total + part[lax.rem(mm - a + n_m, n_m)]
    model[...] = total
    diff = total - meas
    weighted = (diff * prec).astype(BF16)
    own = model[pl.ds(pl.multiple_of(mm * rows, rows), rows), :]
    model_out[...] = own
    own_diff = own - mbuf[0, 0]
    misfit = 0.5 * jnp.sum(mbuf[0, 1] * own_diff * own_diff, keepdims=True)

    vb[...] = dot(rcol_hot, weighted, ((1,), (0,)))
    asked_at = iota((nreq, tile), 0).astype(F32)

    grads = jnp.zeros((nreq, tile), F32)
    for at in range(0, nb, CHUNK):
        left = [
            jnp.where(asked_at == tcol[b : b + 1, :], vb[b : b + 1, :], 0.0).astype(BF16) for b in range(at, at + CHUNK)
        ]
        grads += dot(jnp.concatenate(left, axis=1), sens[at * tile : (at + CHUNK) * tile, :], ((1,), (0,)))

    terms = [grads * flux * tau] + [grads * piece for piece in pieces]
    for c in range(nclass):
        here = cls == c
        for p, term in enumerate(terms):
            srows[pl.ds(p * nclass + c, 1), :] = jnp.sum(jnp.where(here, term, 0.0), axis=0, keepdims=True)
    sums = jnp.sum(srows[...], axis=1, keepdims=True)
    diagonal = iota((nclass, tile), 0) == iota((nclass, tile), 1)
    lines = []
    for p in range(1 + pools):
        line = jnp.sum(jnp.where(diagonal, sums[p * nclass : (p + 1) * nclass], 0.0), axis=0, keepdims=True)
        if p == 0:
            line = jnp.where(iota((1, tile), 1) == nclass, misfit, line)
        lines.append(line)
    share = jnp.concatenate(lines, axis=0)
    back = []
    for e in range(n_s):
        to = grecv if e == 0 else gsend
        to[e, 0:cap, :] = grads[e * cap : (e + 1) * cap]
        to[e, cap:, :] = share
        if e:
            back.append(remote(gsend.at[e], grecv.at[e], s_g.at[e], r_g.at[e], snd_dev(e)))
            back[-1].start()
    if direct:
        tsend[...] = share
        last = [
            remote(tsend, trecv.at[e, f], s_t.at[e, f], r_t.at[e, f], snd_dev(e) | map_dev(f))
            for e in range(n_s)
            for f in range(1, n_m)
        ]
        for c in last:
            c.start()
    for c in back:
        c.wait_recv()
    share = grecv[0, cap:, :]
    for e in range(1, n_s):
        share = share + grecv[e, cap:, :]
    if not direct:
        tsend[...] = share
        last = [remote(tsend, trecv.at[0, f], s_t.at[0, f], r_t.at[0, f], map_dev(f)) for f in range(1, n_m)]
        for c in last:
            c.start()

    for e in range(n_s):
        vecs[0, pl.ds(e * cap, cap), :] = grecv[e, 0:cap, :]
    hi, mid, low = split3(vecs[0])
    placed = (dot(sel, hi, ((0,), (0,))) + dot(sel, mid, ((0,), (0,)))) + dot(sel, low, ((0,), (0,)))
    fg[...] = placed
    for t in range(tiles):
        grad_out[:, pl.ds(t * tile, tile)] = fg[pl.ds(slots * t, slots), :]

    for c in last:
        c.wait_recv()
    for e in range(trecv.shape[0]):
        for f in range(1, n_m):
            share = share + trecv[e, f]
    class_out[0:1, :] = share[0:1, :nclass] + q_v[...] / PRIOR_VAR
    class_out[1:, :] = share[1:, :nclass] + r_v[...] / PRIOR_VAR
    prior = jnp.sum(q_v[...] * q_v[...], keepdims=True) + jnp.sum(r_v[...] * r_v[...], keepdims=True)
    cost_out[...] = share[0:1, nclass : nclass + 1] + 0.5 * prior / PRIOR_VAR

    for c in req + obs + rep + swap + back + last:
        c.wait_send()


def hand_over(*refs):
    n = len(refs) // 2
    writes = [pltpu.make_async_copy(refs[i], refs[n + i], refs[2 * n].at[i]) for i in range(n)]
    for c in writes:
        c.start()
    for c in writes:
        c.wait()


def pinned(x):
    return pltpu.with_memory_space_constraint(x, pltpu.HBM)


def shards(
    n_s,
    n_m,
    sensitivity_blocks,
    block_placement_table,
    needed_tile_lists,
    location_category,
    ground_warmth_celsius,
    wetness_factor,
    carbon_reservoirs,
    category_sensitivity_effect,
    reservoir_decay_effect,
    measured_anomaly,
    retrieval_precision,
):
    nb, tile, _ = sensitivity_blocks.shape
    slots, cells = ground_warmth_celsius.shape
    pools, nclass = reservoir_decay_effect.shape
    tiles = cells // tile
    cap = needed_tile_lists.shape[1]
    nreq = n_s * cap
    rows = measured_anomaly.shape[0]
    allrows = rows * n_m
    hbm = pl.BlockSpec(memory_space=pltpu.HBM)
    vmem = pl.BlockSpec(memory_space=pltpu.VMEM)
    results = (
        jax.ShapeDtypeStruct((rows, tile), F32),
        jax.ShapeDtypeStruct((slots, cells), F32),
        jax.ShapeDtypeStruct((1 + pools, nclass), F32),
        jax.ShapeDtypeStruct((1, 1), F32),
    )
    smem = pl.BlockSpec(memory_space=pltpu.SMEM)
    sem = pltpu.SemaphoreType.DMA
    blocks = nb * tile
    stage = n_s if is_direct(n_s, n_m) else 1
    outs = pl.pallas_call(
        functools.partial(kernel, n_s, n_m),
        out_shape=results,
        in_specs=[hbm, hbm, smem, hbm, hbm, hbm, hbm, smem, smem, hbm, hbm, hbm, hbm],
        out_specs=(vmem,) * 4,
        scratch_shapes=[
            pltpu.VMEM((3, nb), jnp.int32),
            pltpu.VMEM((1, nclass), F32),
            pltpu.VMEM((pools, nclass), F32),
            pltpu.VMEM((nb, tile), F32),
            pltpu.VMEM((blocks, tile), BF16),
            pltpu.VMEM((tiles, tile), jnp.int32),
            pltpu.VMEM((slots, cells), F32),
            pltpu.VMEM((slots, cells), F32),
            pltpu.VMEM((pools, cells), F32),
            pltpu.VMEM((tiles * slots, tile), F32),
            pltpu.VMEM((tiles * slots, tile), F32),
            pltpu.VMEM((tiles * 4, tile), F32),
            pltpu.VMEM((n_s, cap, tile), jnp.int32),
            pltpu.VMEM((n_s, cap, tile), jnp.int32),
            pltpu.VMEM((n_s, 2 * cap, tile), F32),
            pltpu.VMEM((n_s, 2 * cap, tile), F32),
            pltpu.VMEM((n_m, 2, rows, tile), F32),
            pltpu.VMEM((n_m, allrows, tile), F32),
            pltpu.VMEM((n_s, cap + 1 + pools, tile), F32),
            pltpu.VMEM((n_s, cap + 1 + pools, tile), F32),
            pltpu.VMEM((1 + pools, tile), F32),
            pltpu.VMEM((stage, n_m, 1 + pools, tile), F32),
            pltpu.VMEM((2, nreq, tile), jnp.int32),
            pltpu.VMEM((2, nreq, tile), F32),
            pltpu.VMEM((nb, tile), F32),
            pltpu.VMEM((nb, tile), F32),
            pltpu.VMEM((allrows, tile), F32),
            pltpu.VMEM((tiles * slots, tile), F32),
            pltpu.VMEM(((1 + pools) * nclass, tile), F32),
            sem((10,)),
            sem((n_s,)),
            sem((n_s,)),
            sem((n_s,)),
            sem((n_s,)),
            sem((n_m,)),
            sem((n_m,)),
            sem((n_m,)),
            sem((n_m,)),
            sem((n_s,)),
            sem((n_s,)),
            sem((stage, n_m)),
            sem((stage, n_m)),
        ],
        compiler_params=pltpu.CompilerParams(
            collective_id=0, has_side_effects=True, vmem_limit_bytes=24 * 1024 * 1024
        ),
        cost_estimate=pl.CostEstimate(
            flops=2 * blocks * tile * (allrows + nreq), bytes_accessed=2 * blocks * tile, transcendentals=4 * nreq * tile
        ),
        name="inversion",
    )(
        pinned(sensitivity_blocks.reshape(blocks, tile)),
        pinned(block_placement_table),
        pinned(needed_tile_lists.T),
        pinned(location_category.reshape(tiles, tile)),
        pinned(ground_warmth_celsius),
        pinned(wetness_factor),
        pinned(carbon_reservoirs),
        category_sensitivity_effect,
        reservoir_decay_effect,
        pinned(category_sensitivity_effect.reshape(1, nclass)),
        pinned(reservoir_decay_effect),
        pinned(measured_anomaly),
        pinned(retrieval_precision),
    )
    model, grad, classes, cost = pl.pallas_call(
        hand_over,
        out_shape=results,
        in_specs=[vmem] * 4,
        out_specs=(hbm,) * 4,
        scratch_shapes=[sem((4,))],
        name="results",
    )(*outs)
    return model, grad, classes, cost.reshape(())


def solution(mesh):
    in_specs = (
        P(("snd", "map"), None, None),
        P(None, ("snd", "map")),
        P(("snd", "map"), None),
        P("map"),
        P("snd", "map"),
        P("snd", "map"),
        P(None, "map"),
        P(),
        P(),
        P(("snd", "map"), None),
        P(("snd", "map"), None),
    )
    out_specs = (P(("snd", "map"), None), P("snd", "map"), P(), P())
    return jax.shard_map(
        functools.partial(shards, mesh.shape["snd"], mesh.shape["map"]),
        mesh=mesh,
        in_specs=in_specs,
        out_specs=out_specs,
        check_vma=False,
    )
```

```python
import functools

import jax
import jax.numpy as jnp
from jax import lax
from jax.experimental import pallas as pl
from jax.experimental.pallas import tpu as pltpu
from jax.sharding import PartitionSpec as P

BASELINE_CELSIUS = 15.0
LOG_BASE_Q = 0.6931471805599453
PRIOR_VAR = 0.09
RATES = (0.6, 0.25, 0.1)
CHUNK = 16
F32 = jnp.float32
BF16 = jnp.bfloat16


def split3(x):
    hi = x.astype(BF16)
    rest = x - hi.astype(F32)
    mid = rest.astype(BF16)
    low = (rest - mid.astype(F32)).astype(BF16)
    return hi, mid, low


def dot(a, b, dims):
    return lax.dot_general(a, b, (dims, ((), ())), preferred_element_type=F32)


def onehot(mask):
    return jnp.where(mask, 1.0, 0.0).astype(BF16)


def pick(sel, x):
    hi, mid, low = split3(x)
    return (dot(sel, hi, ((1,), (0,))) + dot(sel, mid, ((1,), (0,)))) + dot(sel, low, ((1,), (0,)))


def iota(shape, dim):
    return lax.broadcasted_iota(jnp.int32, shape, dim)


def is_direct(n_s, n_m):
    return n_s * n_m <= 64


def kernel(
    n_s, n_m, sens_hbm, table_hbm, lists, cat_hbm, warm_hbm, wet_hbm, carb_hbm, q_s, r_s, q_hbm, r_hbm, meas_hbm,
    prec_hbm,
    model_out, grad_out, class_out, cost_out, table, q_v, r_v, vb, sens, cat, warm_in, wet_in, carb_in, warm, wet, carb,
    req_send, req_recv, rep_send, rep_recv, mbuf, part, gsend, grecv, tsend, trecv,
    ids, vecs, tcol, rcol, model, fg, srows,
    local_sem, s_req, r_req, s_rep, r_rep, s_m, r_m, s_p, r_p, s_g, r_g, s_t, r_t,
):
    cap = lists.shape[0]
    nreq = n_s * cap
    slots = warm_hbm.shape[0]
    tiles = cat.shape[0]
    nclass = q_s.shape[0]
    pools = carb_hbm.shape[0]
    rows = meas_hbm.shape[0]
    allrows = rows * n_m
    nb = table.shape[1]
    tile = sens.shape[1]
    me = lax.axis_index("snd")
    mm = lax.axis_index("map")
    snd_dev = lambda e: {"snd": lax.rem(me + e + n_s, n_s)}
    map_dev = lambda f: {"map": lax.rem(mm + f + n_m, n_m)}

    def remote(src, dst, ss, rs, dev):
        return pltpu.make_async_remote_copy(
            src_ref=src, dst_ref=dst, send_sem=ss, recv_sem=rs, device_id=dev, device_id_type=pl.DeviceIdType.MESH
        )

    barrier = pltpu.get_barrier_semaphore()
    direct = is_direct(n_s, n_m)
    others = [(e, f) for e in range(n_s) for f in range(n_m) if e + f and (direct or e == 0 or f == 0)]
    for e, f in others:
        pl.semaphore_signal(barrier, inc=1, device_id=snd_dev(e) | map_dev(f), device_id_type=pl.DeviceIdType.MESH)

    loads = [
        pltpu.make_async_copy(src, dst, local_sem.at[i])
        for i, (src, dst) in enumerate(
            [
                (warm_hbm, warm_in),
                (wet_hbm, wet_in),
                (table_hbm, table),
                (carb_hbm, carb_in),
                (cat_hbm, cat),
                (meas_hbm, mbuf.at[0, 0]),
                (prec_hbm, mbuf.at[0, 1]),
                (q_hbm, q_v),
                (r_hbm, r_v),
                (sens_hbm, sens),
            ]
        )
    ]
    for load in loads:
        load.start()

    row_in = iota((cap, tile), 0)
    for e in range(n_s):
        owner = lax.rem(me + e, n_s)
        whole_id = jnp.full((cap, tile), -1, jnp.int32)
        spot = jnp.full((cap, tile), -1, jnp.int32)
        tile_id = jnp.full((cap, tile), -1, jnp.int32)
        for k in range(cap):
            asked = lists[k, owner]
            t = lax.rem(asked, tiles)
            here = row_in == k
            whole_id = jnp.where(here, jnp.where(asked < 0, -1, owner * (slots * tiles) + asked), whole_id)
            spot = jnp.where(here, t * slots + lax.div(asked, tiles), spot)
            tile_id = jnp.where(here, t, tile_id)
        if e == 0:
            req_recv[0] = spot
        else:
            req_send[e] = spot
        ids[0, pl.ds(e * cap, cap), :] = whole_id
        ids[1, pl.ds(e * cap, cap), :] = tile_id

    pl.semaphore_wait(barrier, len(others))

    req = [remote(req_send.at[e], req_recv.at[e], s_req.at[e], r_req.at[e], snd_dev(e)) for e in range(1, n_s)]
    for c in req:
        c.start()
    carb[...] = jnp.zeros_like(carb)
    for load in loads[:3]:
        load.wait()
    for t in range(tiles):
        lanes = pl.ds(t * tile, tile)
        warm[pl.ds(slots * t, slots), :] = warm_in[:, lanes]
        wet[pl.ds(slots * t, slots), :] = wet_in[:, lanes]
    observed = jnp.concatenate(split3(warm[...]) + split3(wet[...]), axis=1)

    block_row = table[0:1, :]
    block_id = table[2:3, :] * tiles + table[1:2, :]
    asked_hot = onehot(ids[0][:, :nb] == block_id)
    row_hot = onehot(iota((allrows, nb), 0) == block_row)
    tcol[...] = dot(asked_hot, iota((nreq, tile), 0).astype(F32).astype(BF16), ((0,), (0,)))
    rcol[...] = dot(row_hot, iota((allrows, tile), 0).astype(F32).astype(BF16), ((0,), (0,)))

    for c in req:
        c.wait_recv()
    for e in range(n_s):
        ids[0, pl.ds(e * cap, cap), :] = req_recv[e]
    sel = onehot(ids[0] == iota((nreq, tile), 1))
    every = dot(sel, observed, ((1,), (0,)))
    cut = [every[:, i * tile : (i + 1) * tile] for i in range(6)]
    out_warm = (cut[0] + cut[1]) + cut[2]
    out_wet = (cut[3] + cut[4]) + cut[5]
    rep = []
    for e in range(n_s):
        to = rep_recv if e == 0 else rep_send
        to[e, 0:cap, :] = out_warm[e * cap : (e + 1) * cap]
        to[e, cap : 2 * cap, :] = out_wet[e * cap : (e + 1) * cap]
        if e:
            rep.append(remote(rep_send.at[e], rep_recv.at[e], s_rep.at[e], r_rep.at[e], snd_dev(-e)))
            rep[-1].start()
    for load in loads[5:7]:
        load.wait()
    obs = [remote(mbuf.at[0], mbuf.at[f], s_m.at[f], r_m.at[f], map_dev(f)) for f in range(1, n_m)]
    for c in obs:
        c.start()

    for load in loads[3:5]:
        load.wait()
    for t in range(tiles):
        carb[pl.ds(4 * t, pools), :] = carb_in[:, pl.ds(t * tile, tile)]
    tile_id = ids[1]
    cls = dot(onehot(tile_id[:, :tiles] == iota((nreq, tiles), 1)), cat[...].astype(F32).astype(BF16), ((1,), (0,)))
    cls = cls.astype(jnp.int32)
    wide = jnp.concatenate([tile_id] * (4 * tiles // tile), axis=1)
    wide_at = iota((nreq, 4 * tiles), 1)
    log_q = jnp.zeros((nreq, tile), F32)
    effects = [jnp.zeros((nreq, tile), F32) for _ in range(pools)]
    for c in range(nclass):
        here = cls == c
        log_q = jnp.where(here, q_s[c], log_q)
        for p in range(pools):
            effects[p] = jnp.where(here, r_s[p, c], effects[p])
    log_q = LOG_BASE_Q + log_q
    held = []
    for p in range(pools):
        carbon = pick(onehot(wide * 4 + p == wide_at), carb[...])
        held.append(RATES[p] * jnp.exp(effects[p]) * carbon)

    tcol_hot = onehot(tcol[:, :nreq] == iota((nb, nreq), 1).astype(F32))
    for c in rep:
        c.wait_recv()
    for e in range(n_s):
        vecs[0, pl.ds(e * cap, cap), :] = rep_recv[e, 0:cap, :]
        vecs[1, pl.ds(e * cap, cap), :] = rep_recv[e, cap : 2 * cap, :]

    tau = (vecs[0] - BASELINE_CELSIUS) / 10.0
    modifier = jnp.exp(log_q * tau) * vecs[1]
    pieces = [h * modifier for h in held]
    flux = pieces[0] + pieces[1] + pieces[2]
    flux_low = flux.astype(BF16)

    vecs_b = dot(tcol_hot, flux_low, ((1,), (0,)))
    model_at = iota((allrows, tile), 0).astype(F32)
    vb[...] = vecs_b
    loads[9].wait()

    partial = jnp.zeros((allrows, tile), F32)
    for at in range(0, nb, CHUNK):
        left = [
            jnp.where(model_at == rcol[b : b + 1, :], vb[b : b + 1, :], 0.0).astype(BF16) for b in range(at, at + CHUNK)
        ]
        right = [sens[b * tile : (b + 1) * tile, :] for b in range(at, at + CHUNK)]
        partial += dot(jnp.concatenate(left, axis=1), jnp.concatenate(right, axis=1), ((1,), (1,)))
    part[0] = partial

    swap = [remote(part.at[0], part.at[f], s_p.at[f], r_p.at[f], map_dev(f)) for f in range(1, n_m)]
    for c in swap:
        c.start()
    for c in loads[7:9]:
        c.wait()
    for c in obs:
        c.wait_recv()
    meas, prec = [], []
    for a in range(n_m):
        slot = lax.rem(mm - a + n_m, n_m)
        meas.append(mbuf[slot, 0])
        prec.append(mbuf[slot, 1])
    meas = jnp.concatenate(meas, axis=0)
    prec = jnp.concatenate(prec, axis=0)
    rcol_hot = onehot(rcol[:, :allrows] == iota((nb, allrows), 1).astype(F32))
    for c in swap:
        c.wait_recv()
    total = part[lax.rem(mm + n_m, n_m)]
    for a in range(1, n_m):
        total = total + part[lax.rem(mm - a + n_m, n_m)]
    model[...] = total
    diff = total - meas
    weighted = (diff * prec).astype(BF16)
    own = model[pl.ds(pl.multiple_of(mm * rows, rows), rows), :]
    model_out[...] = own
    own_diff = own - mbuf[0, 0]
    misfit = 0.5 * jnp.sum(mbuf[0, 1] * own_diff * own_diff, keepdims=True)

    vb[...] = dot(rcol_hot, weighted, ((1,), (0,)))
    asked_at = iota((nreq, tile), 0).astype(F32)

    grads = jnp.zeros((nreq, tile), F32)
    for at in range(0, nb, CHUNK):
        left = [
            jnp.where(asked_at == tcol[b : b + 1, :], vb[b : b + 1, :], 0.0).astype(BF16) for b in range(at, at + CHUNK)
        ]
        grads += dot(jnp.concatenate(left, axis=1), sens[at * tile : (at + CHUNK) * tile, :], ((1,), (0,)))

    terms = [grads * flux * tau] + [grads * piece for piece in pieces]
    for c in range(nclass):
        here = cls == c
        for p, term in enumerate(terms):
            srows[pl.ds(p * nclass + c, 1), :] = jnp.sum(jnp.where(here, term, 0.0), axis=0, keepdims=True)
    sums = jnp.sum(srows[...], axis=1, keepdims=True)
    diagonal = iota((nclass, tile), 0) == iota((nclass, tile), 1)
    lines = []
    for p in range(1 + pools):
        line = jnp.sum(jnp.where(diagonal, sums[p * nclass : (p + 1) * nclass], 0.0), axis=0, keepdims=True)
        if p == 0:
            line = jnp.where(iota((1, tile), 1) == nclass, misfit, line)
        lines.append(line)
    share = jnp.concatenate(lines, axis=0)
    back = []
    for e in range(n_s):
        to = grecv if e == 0 else gsend
        to[e, 0:cap, :] = grads[e * cap : (e + 1) * cap]
        to[e, cap:, :] = share
        if e:
            back.append(remote(gsend.at[e], grecv.at[e], s_g.at[e], r_g.at[e], snd_dev(e)))
            back[-1].start()
    if direct:
        tsend[...] = share
        last = [
            remote(tsend, trecv.at[e, f], s_t.at[e, f], r_t.at[e, f], snd_dev(e) | map_dev(f))
            for e in range(n_s)
            for f in range(1, n_m)
        ]
        for c in last:
            c.start()
    for c in back:
        c.wait_recv()
    share = grecv[0, cap:, :]
    for e in range(1, n_s):
        share = share + grecv[e, cap:, :]
    if not direct:
        tsend[...] = share
        last = [remote(tsend, trecv.at[0, f], s_t.at[0, f], r_t.at[0, f], map_dev(f)) for f in range(1, n_m)]
        for c in last:
            c.start()

    for e in range(n_s):
        vecs[0, pl.ds(e * cap, cap), :] = grecv[e, 0:cap, :]
    hi, mid, low = split3(vecs[0])
    placed = (dot(sel, hi, ((0,), (0,))) + dot(sel, mid, ((0,), (0,)))) + dot(sel, low, ((0,), (0,)))
    fg[...] = placed
    for t in range(tiles):
        grad_out[:, pl.ds(t * tile, tile)] = fg[pl.ds(slots * t, slots), :]

    for c in last:
        c.wait_recv()
    for e in range(trecv.shape[0]):
        for f in range(1, n_m):
            share = share + trecv[e, f]
    class_out[0:1, :] = share[0:1, :nclass] + q_v[...] / PRIOR_VAR
    class_out[1:, :] = share[1:, :nclass] + r_v[...] / PRIOR_VAR
    prior = jnp.sum(q_v[...] * q_v[...], keepdims=True) + jnp.sum(r_v[...] * r_v[...], keepdims=True)
    cost_out[...] = share[0:1, nclass : nclass + 1] + 0.5 * prior / PRIOR_VAR

    for c in req + obs + rep + swap + back + last:
        c.wait_send()


def hand_over(*refs):
    n = len(refs) // 2
    writes = [pltpu.make_async_copy(refs[i], refs[n + i], refs[2 * n].at[i]) for i in range(n)]
    for c in writes:
        c.start()
    for c in writes:
        c.wait()


def pinned(x):
    return pltpu.with_memory_space_constraint(x, pltpu.HBM)


def shards(
    n_s,
    n_m,
    sensitivity_blocks,
    block_placement_table,
    needed_tile_lists,
    location_category,
    ground_warmth_celsius,
    wetness_factor,
    carbon_reservoirs,
    category_sensitivity_effect,
    reservoir_decay_effect,
    measured_anomaly,
    retrieval_precision,
):
    nb, tile, _ = sensitivity_blocks.shape
    slots, cells = ground_warmth_celsius.shape
    pools, nclass = reservoir_decay_effect.shape
    tiles = cells // tile
    cap = needed_tile_lists.shape[1]
    nreq = n_s * cap
    rows = measured_anomaly.shape[0]
    allrows = rows * n_m
    hbm = pl.BlockSpec(memory_space=pltpu.HBM)
    vmem = pl.BlockSpec(memory_space=pltpu.VMEM)
    results = (
        jax.ShapeDtypeStruct((rows, tile), F32),
        jax.ShapeDtypeStruct((slots, cells), F32),
        jax.ShapeDtypeStruct((1 + pools, nclass), F32),
        jax.ShapeDtypeStruct((1, 1), F32),
    )
    smem = pl.BlockSpec(memory_space=pltpu.SMEM)
    sem = pltpu.SemaphoreType.DMA
    blocks = nb * tile
    stage = n_s if is_direct(n_s, n_m) else 1
    outs = pl.pallas_call(
        functools.partial(kernel, n_s, n_m),
        out_shape=results,
        in_specs=[hbm, hbm, smem, hbm, hbm, hbm, hbm, smem, smem, hbm, hbm, hbm, hbm],
        out_specs=(vmem,) * 4,
        scratch_shapes=[
            pltpu.VMEM((3, nb), jnp.int32),
            pltpu.VMEM((1, nclass), F32),
            pltpu.VMEM((pools, nclass), F32),
            pltpu.VMEM((nb, tile), F32),
            pltpu.VMEM((blocks, tile), BF16),
            pltpu.VMEM((tiles, tile), jnp.int32),
            pltpu.VMEM((slots, cells), F32),
            pltpu.VMEM((slots, cells), F32),
            pltpu.VMEM((pools, cells), F32),
            pltpu.VMEM((tiles * slots, tile), F32),
            pltpu.VMEM((tiles * slots, tile), F32),
            pltpu.VMEM((tiles * 4, tile), F32),
            pltpu.VMEM((n_s, cap, tile), jnp.int32),
            pltpu.VMEM((n_s, cap, tile), jnp.int32),
            pltpu.VMEM((n_s, 2 * cap, tile), F32),
            pltpu.VMEM((n_s, 2 * cap, tile), F32),
            pltpu.VMEM((n_m, 2, rows, tile), F32),
            pltpu.VMEM((n_m, allrows, tile), F32),
            pltpu.VMEM((n_s, cap + 1 + pools, tile), F32),
            pltpu.VMEM((n_s, cap + 1 + pools, tile), F32),
            pltpu.VMEM((1 + pools, tile), F32),
            pltpu.VMEM((stage, n_m, 1 + pools, tile), F32),
            pltpu.VMEM((2, nreq, tile), jnp.int32),
            pltpu.VMEM((2, nreq, tile), F32),
            pltpu.VMEM((nb, tile), F32),
            pltpu.VMEM((nb, tile), F32),
            pltpu.VMEM((allrows, tile), F32),
            pltpu.VMEM((tiles * slots, tile), F32),
            pltpu.VMEM(((1 + pools) * nclass, tile), F32),
            sem((10,)),
            sem((n_s,)),
            sem((n_s,)),
            sem((n_s,)),
            sem((n_s,)),
            sem((n_m,)),
            sem((n_m,)),
            sem((n_m,)),
            sem((n_m,)),
            sem((n_s,)),
            sem((n_s,)),
            sem((stage, n_m)),
            sem((stage, n_m)),
        ],
        compiler_params=pltpu.CompilerParams(
            collective_id=0, has_side_effects=True, vmem_limit_bytes=24 * 1024 * 1024
        ),
        cost_estimate=pl.CostEstimate(
            flops=2 * blocks * tile * (allrows + nreq), bytes_accessed=2 * blocks * tile, transcendentals=4 * nreq * tile
        ),
        name="inversion",
    )(
        pinned(sensitivity_blocks.reshape(blocks, tile)),
        pinned(block_placement_table),
        pinned(needed_tile_lists.T),
        pinned(location_category.reshape(tiles, tile)),
        pinned(ground_warmth_celsius),
        pinned(wetness_factor),
        pinned(carbon_reservoirs),
        category_sensitivity_effect,
        reservoir_decay_effect,
        pinned(category_sensitivity_effect.reshape(1, nclass)),
        pinned(reservoir_decay_effect),
        pinned(measured_anomaly),
        pinned(retrieval_precision),
    )
    model, grad, classes, cost = pl.pallas_call(
        hand_over,
        out_shape=results,
        in_specs=[vmem] * 4,
        out_specs=(hbm,) * 4,
        scratch_shapes=[sem((4,))],
        compiler_params=pltpu.CompilerParams(vmem_limit_bytes=2 * 1024 * 1024),
        name="results",
    )(*outs)
    return model, grad, classes, cost.reshape(())


def solution(mesh):
    in_specs = (
        P(("snd", "map"), None, None),
        P(None, ("snd", "map")),
        P(("snd", "map"), None),
        P("map"),
        P("snd", "map"),
        P("snd", "map"),
        P(None, "map"),
        P(),
        P(),
        P(("snd", "map"), None),
        P(("snd", "map"), None),
    )
    out_specs = (P(("snd", "map"), None), P("snd", "map"), P(), P())
    return jax.shard_map(
        functools.partial(shards, mesh.shape["snd"], mesh.shape["map"]),
        mesh=mesh,
        in_specs=in_specs,
        out_specs=out_specs,
        check_vma=False,
    )
```

```python
import functools

import jax
import jax.numpy as jnp
from jax import lax
from jax.experimental import pallas as pl
from jax.experimental.pallas import tpu as pltpu
from jax.sharding import PartitionSpec as P

BASELINE_CELSIUS = 15.0
LOG_BASE_Q = 0.6931471805599453
PRIOR_VAR = 0.09
RATES = (0.6, 0.25, 0.1)
CHUNK = 16
F32 = jnp.float32
BF16 = jnp.bfloat16


def split3(x):
    hi = x.astype(BF16)
    rest = x - hi.astype(F32)
    mid = rest.astype(BF16)
    low = (rest - mid.astype(F32)).astype(BF16)
    return hi, mid, low


def dot(a, b, dims):
    return lax.dot_general(a, b, (dims, ((), ())), preferred_element_type=F32)


def onehot(mask):
    return jnp.where(mask, 1.0, 0.0).astype(BF16)


def pick(sel, x):
    hi, mid, low = split3(x)
    return (dot(sel, hi, ((1,), (0,))) + dot(sel, mid, ((1,), (0,)))) + dot(sel, low, ((1,), (0,)))


def iota(shape, dim):
    return lax.broadcasted_iota(jnp.int32, shape, dim)


def is_direct(n_s, n_m):
    return n_s * n_m <= 64


def kernel(
    n_s, n_m, sens_hbm, table_hbm, lists, cat_hbm, warm_hbm, wet_hbm, carb_hbm, q_s, r_s, q_hbm, r_hbm, meas_hbm,
    prec_hbm,
    model_out, grad_out, class_out, cost_out, table, q_v, r_v, vb, sens, cat, warm_in, wet_in, carb_in, warm, wet, carb,
    req_send, req_recv, rep_send, rep_recv, mbuf, part, gsend, grecv, tsend, trecv,
    ids, vecs, tcol, rcol, model, fg, srows,
    local_sem, s_req, r_req, s_rep, r_rep, s_m, r_m, s_p, r_p, s_g, r_g, s_t, r_t,
):
    cap = lists.shape[0]
    nreq = n_s * cap
    slots = warm_hbm.shape[0]
    tiles = cat.shape[0]
    nclass = q_s.shape[0]
    pools = carb_hbm.shape[0]
    rows = meas_hbm.shape[0]
    allrows = rows * n_m
    nb = table.shape[1]
    tile = sens.shape[1]
    me = lax.axis_index("snd")
    mm = lax.axis_index("map")
    snd_dev = lambda e: {"snd": lax.rem(me + e + n_s, n_s)}
    map_dev = lambda f: {"map": lax.rem(mm + f + n_m, n_m)}

    def remote(src, dst, ss, rs, dev):
        return pltpu.make_async_remote_copy(
            src_ref=src, dst_ref=dst, send_sem=ss, recv_sem=rs, device_id=dev, device_id_type=pl.DeviceIdType.MESH
        )

    barrier = pltpu.get_barrier_semaphore()
    direct = is_direct(n_s, n_m)
    others = [(e, f) for e in range(n_s) for f in range(n_m) if e + f and (direct or e == 0 or f == 0)]
    for e, f in others:
        pl.semaphore_signal(barrier, inc=1, device_id=snd_dev(e) | map_dev(f), device_id_type=pl.DeviceIdType.MESH)

    loads = [
        pltpu.make_async_copy(src, dst, local_sem.at[i])
        for i, (src, dst) in enumerate(
            [
                (warm_hbm, warm_in),
                (wet_hbm, wet_in),
                (table_hbm, table),
                (carb_hbm, carb_in),
                (cat_hbm, cat),
                (meas_hbm, mbuf.at[0, 0]),
                (prec_hbm, mbuf.at[0, 1]),
                (q_hbm, q_v),
                (r_hbm, r_v),
                (sens_hbm, sens),
            ]
        )
    ]
    for load in loads:
        load.start()

    row_in = iota((cap, tile), 0)
    for e in range(n_s):
        owner = lax.rem(me + e, n_s)
        whole_id = jnp.full((cap, tile), -1, jnp.int32)
        spot = jnp.full((cap, tile), -1, jnp.int32)
        tile_id = jnp.full((cap, tile), -1, jnp.int32)
        for k in range(cap):
            asked = lists[k, owner]
            t = lax.rem(asked, tiles)
            here = row_in == k
            whole_id = jnp.where(here, jnp.where(asked < 0, -1, owner * (slots * tiles) + asked), whole_id)
            spot = jnp.where(here, t * slots + lax.div(asked, tiles), spot)
            tile_id = jnp.where(here, t, tile_id)
        if e == 0:
            req_recv[0] = spot
        else:
            req_send[e] = spot
        ids[0, pl.ds(e * cap, cap), :] = whole_id
        ids[1, pl.ds(e * cap, cap), :] = tile_id

    pl.semaphore_wait(barrier, len(others))

    req = [remote(req_send.at[e], req_recv.at[e], s_req.at[e], r_req.at[e], snd_dev(e)) for e in range(1, n_s)]
    for c in req:
        c.start()
    carb[...] = jnp.zeros_like(carb)
    for load in loads[:3]:
        load.wait()
    for t in range(tiles):
        lanes = pl.ds(t * tile, tile)
        warm[pl.ds(slots * t, slots), :] = warm_in[:, lanes]
        wet[pl.ds(slots * t, slots), :] = wet_in[:, lanes]
    observed = jnp.concatenate(split3(warm[...]) + split3(wet[...]), axis=1)

    block_row = table[0:1, :]
    block_id = table[2:3, :] * tiles + table[1:2, :]
    asked_hot = onehot(ids[0][:, :nb] == block_id)
    row_hot = onehot(iota((allrows, nb), 0) == block_row)
    tcol[...] = dot(asked_hot, iota((nreq, tile), 0).astype(F32).astype(BF16), ((0,), (0,)))
    rcol[...] = dot(row_hot, iota((allrows, tile), 0).astype(F32).astype(BF16), ((0,), (0,)))

    for c in req:
        c.wait_recv()
    for e in range(n_s):
        ids[0, pl.ds(e * cap, cap), :] = req_recv[e]
    sel = onehot(ids[0] == iota((nreq, tile), 1))
    every = dot(sel, observed, ((1,), (0,)))
    cut = [every[:, i * tile : (i + 1) * tile] for i in range(6)]
    out_warm = (cut[0] + cut[1]) + cut[2]
    out_wet = (cut[3] + cut[4]) + cut[5]
    rep = []
    for e in range(n_s):
        to = rep_recv if e == 0 else rep_send
        to[e, 0:cap, :] = out_warm[e * cap : (e + 1) * cap]
        to[e, cap : 2 * cap, :] = out_wet[e * cap : (e + 1) * cap]
        if e:
            rep.append(remote(rep_send.at[e], rep_recv.at[e], s_rep.at[e], r_rep.at[e], snd_dev(-e)))
            rep[-1].start()
    for load in loads[5:7]:
        load.wait()
    obs = [remote(mbuf.at[0], mbuf.at[f], s_m.at[f], r_m.at[f], map_dev(f)) for f in range(1, n_m)]
    for c in obs:
        c.start()

    for load in loads[3:5]:
        load.wait()
    for t in range(tiles):
        carb[pl.ds(4 * t, pools), :] = carb_in[:, pl.ds(t * tile, tile)]
    tile_id = ids[1]
    cls = dot(onehot(tile_id[:, :tiles] == iota((nreq, tiles), 1)), cat[...].astype(F32).astype(BF16), ((1,), (0,)))
    cls = cls.astype(jnp.int32)
    wide = jnp.concatenate([tile_id] * (4 * tiles // tile), axis=1)
    wide_at = iota((nreq, 4 * tiles), 1)
    log_q = jnp.zeros((nreq, tile), F32)
    effects = [jnp.zeros((nreq, tile), F32) for _ in range(pools)]
    for c in range(nclass):
        here = cls == c
        log_q = jnp.where(here, q_s[c], log_q)
        for p in range(pools):
            effects[p] = jnp.where(here, r_s[p, c], effects[p])
    log_q = LOG_BASE_Q + log_q
    held = []
    for p in range(pools):
        carbon = pick(onehot(wide * 4 + p == wide_at), carb[...])
        held.append(RATES[p] * jnp.exp(effects[p]) * carbon)

    tcol_hot = onehot(tcol[:, :nreq] == iota((nb, nreq), 1).astype(F32))
    for c in rep:
        c.wait_recv()
    for e in range(n_s):
        vecs[0, pl.ds(e * cap, cap), :] = rep_recv[e, 0:cap, :]
        vecs[1, pl.ds(e * cap, cap), :] = rep_recv[e, cap : 2 * cap, :]

    tau = (vecs[0] - BASELINE_CELSIUS) / 10.0
    modifier = jnp.exp(log_q * tau) * vecs[1]
    pieces = [h * modifier for h in held]
    flux = pieces[0] + pieces[1] + pieces[2]
    flux_low = flux.astype(BF16)

    vecs_b = dot(tcol_hot, flux_low, ((1,), (0,)))
    model_at = iota((allrows, tile), 0).astype(F32)
    vb[...] = vecs_b
    loads[9].wait()

    partial = jnp.zeros((tile, allrows), F32)
    for at in range(0, nb, CHUNK):
        left = [
            jnp.where(model_at == rcol[b : b + 1, :], vb[b : b + 1, :], 0.0).astype(BF16) for b in range(at, at + CHUNK)
        ]
        right = [sens[b * tile : (b + 1) * tile, :] for b in range(at, at + CHUNK)]
        partial += dot(jnp.concatenate(right, axis=1), jnp.concatenate(left, axis=1), ((1,), (1,)))
    part[0] = partial.T

    swap = [remote(part.at[0], part.at[f], s_p.at[f], r_p.at[f], map_dev(f)) for f in range(1, n_m)]
    for c in swap:
        c.start()
    for c in loads[7:9]:
        c.wait()
    for c in obs:
        c.wait_recv()
    meas, prec = [], []
    for a in range(n_m):
        slot = lax.rem(mm - a + n_m, n_m)
        meas.append(mbuf[slot, 0])
        prec.append(mbuf[slot, 1])
    meas = jnp.concatenate(meas, axis=0)
    prec = jnp.concatenate(prec, axis=0)
    rcol_hot = onehot(rcol[:, :allrows] == iota((nb, allrows), 1).astype(F32))
    for c in swap:
        c.wait_recv()
    total = part[lax.rem(mm + n_m, n_m)]
    for a in range(1, n_m):
        total = total + part[lax.rem(mm - a + n_m, n_m)]
    model[...] = total
    diff = total - meas
    weighted = (diff * prec).astype(BF16)
    own = model[pl.ds(pl.multiple_of(mm * rows, rows), rows), :]
    model_out[...] = own
    own_diff = own - mbuf[0, 0]
    misfit = 0.5 * jnp.sum(mbuf[0, 1] * own_diff * own_diff, keepdims=True)

    vb[...] = dot(rcol_hot, weighted, ((1,), (0,)))
    asked_at = iota((nreq, tile), 0).astype(F32)

    grads = jnp.zeros((nreq, tile), F32)
    for at in range(0, nb, CHUNK):
        left = [
            jnp.where(asked_at == tcol[b : b + 1, :], vb[b : b + 1, :], 0.0).astype(BF16) for b in range(at, at + CHUNK)
        ]
        grads += dot(jnp.concatenate(left, axis=1), sens[at * tile : (at + CHUNK) * tile, :], ((1,), (0,)))

    terms = [grads * flux * tau] + [grads * piece for piece in pieces]
    for c in range(nclass):
        here = cls == c
        for p, term in enumerate(terms):
            srows[pl.ds(p * nclass + c, 1), :] = jnp.sum(jnp.where(here, term, 0.0), axis=0, keepdims=True)
    sums = jnp.sum(srows[...], axis=1, keepdims=True)
    diagonal = iota((nclass, tile), 0) == iota((nclass, tile), 1)
    lines = []
    for p in range(1 + pools):
        line = jnp.sum(jnp.where(diagonal, sums[p * nclass : (p + 1) * nclass], 0.0), axis=0, keepdims=True)
        if p == 0:
            line = jnp.where(iota((1, tile), 1) == nclass, misfit, line)
        lines.append(line)
    share = jnp.concatenate(lines, axis=0)
    back = []
    for e in range(n_s):
        to = grecv if e == 0 else gsend
        to[e, 0:cap, :] = grads[e * cap : (e + 1) * cap]
        to[e, cap:, :] = share
        if e:
            back.append(remote(gsend.at[e], grecv.at[e], s_g.at[e], r_g.at[e], snd_dev(e)))
            back[-1].start()
    if direct:
        tsend[...] = share
        last = [
            remote(tsend, trecv.at[e, f], s_t.at[e, f], r_t.at[e, f], snd_dev(e) | map_dev(f))
            for e in range(n_s)
            for f in range(1, n_m)
        ]
        for c in last:
            c.start()
    for c in back:
        c.wait_recv()
    share = grecv[0, cap:, :]
    for e in range(1, n_s):
        share = share + grecv[e, cap:, :]
    if not direct:
        tsend[...] = share
        last = [remote(tsend, trecv.at[0, f], s_t.at[0, f], r_t.at[0, f], map_dev(f)) for f in range(1, n_m)]
        for c in last:
            c.start()

    for e in range(n_s):
        vecs[0, pl.ds(e * cap, cap), :] = grecv[e, 0:cap, :]
    hi, mid, low = split3(vecs[0])
    placed = (dot(sel, hi, ((0,), (0,))) + dot(sel, mid, ((0,), (0,)))) + dot(sel, low, ((0,), (0,)))
    fg[...] = placed
    for t in range(tiles):
        grad_out[:, pl.ds(t * tile, tile)] = fg[pl.ds(slots * t, slots), :]

    for c in last:
        c.wait_recv()
    for e in range(trecv.shape[0]):
        for f in range(1, n_m):
            share = share + trecv[e, f]
    class_out[0:1, :] = share[0:1, :nclass] + q_v[...] / PRIOR_VAR
    class_out[1:, :] = share[1:, :nclass] + r_v[...] / PRIOR_VAR
    prior = jnp.sum(q_v[...] * q_v[...], keepdims=True) + jnp.sum(r_v[...] * r_v[...], keepdims=True)
    cost_out[...] = share[0:1, nclass : nclass + 1] + 0.5 * prior / PRIOR_VAR

    for c in req + obs + rep + swap + back + last:
        c.wait_send()


def hand_over(*refs):
    n = len(refs) // 2
    writes = [pltpu.make_async_copy(refs[i], refs[n + i], refs[2 * n].at[i]) for i in range(n)]
    for c in writes:
        c.start()
    for c in writes:
        c.wait()


def pinned(x):
    return pltpu.with_memory_space_constraint(x, pltpu.HBM)


def shards(
    n_s,
    n_m,
    sensitivity_blocks,
    block_placement_table,
    needed_tile_lists,
    location_category,
    ground_warmth_celsius,
    wetness_factor,
    carbon_reservoirs,
    category_sensitivity_effect,
    reservoir_decay_effect,
    measured_anomaly,
    retrieval_precision,
):
    nb, tile, _ = sensitivity_blocks.shape
    slots, cells = ground_warmth_celsius.shape
    pools, nclass = reservoir_decay_effect.shape
    tiles = cells // tile
    cap = needed_tile_lists.shape[1]
    nreq = n_s * cap
    rows = measured_anomaly.shape[0]
    allrows = rows * n_m
    hbm = pl.BlockSpec(memory_space=pltpu.HBM)
    vmem = pl.BlockSpec(memory_space=pltpu.VMEM)
    results = (
        jax.ShapeDtypeStruct((rows, tile), F32),
        jax.ShapeDtypeStruct((slots, cells), F32),
        jax.ShapeDtypeStruct((1 + pools, nclass), F32),
        jax.ShapeDtypeStruct((1, 1), F32),
    )
    smem = pl.BlockSpec(memory_space=pltpu.SMEM)
    sem = pltpu.SemaphoreType.DMA
    blocks = nb * tile
    stage = n_s if is_direct(n_s, n_m) else 1
    outs = pl.pallas_call(
        functools.partial(kernel, n_s, n_m),
        out_shape=results,
        in_specs=[hbm, hbm, smem, hbm, hbm, hbm, hbm, smem, smem, hbm, hbm, hbm, hbm],
        out_specs=(vmem,) * 4,
        scratch_shapes=[
            pltpu.VMEM((3, nb), jnp.int32),
            pltpu.VMEM((1, nclass), F32),
            pltpu.VMEM((pools, nclass), F32),
            pltpu.VMEM((nb, tile), F32),
            pltpu.VMEM((blocks, tile), BF16),
            pltpu.VMEM((tiles, tile), jnp.int32),
            pltpu.VMEM((slots, cells), F32),
            pltpu.VMEM((slots, cells), F32),
            pltpu.VMEM((pools, cells), F32),
            pltpu.VMEM((tiles * slots, tile), F32),
            pltpu.VMEM((tiles * slots, tile), F32),
            pltpu.VMEM((tiles * 4, tile), F32),
            pltpu.VMEM((n_s, cap, tile), jnp.int32),
            pltpu.VMEM((n_s, cap, tile), jnp.int32),
            pltpu.VMEM((n_s, 2 * cap, tile), F32),
            pltpu.VMEM((n_s, 2 * cap, tile), F32),
            pltpu.VMEM((n_m, 2, rows, tile), F32),
            pltpu.VMEM((n_m, allrows, tile), F32),
            pltpu.VMEM((n_s, cap + 1 + pools, tile), F32),
            pltpu.VMEM((n_s, cap + 1 + pools, tile), F32),
            pltpu.VMEM((1 + pools, tile), F32),
            pltpu.VMEM((stage, n_m, 1 + pools, tile), F32),
            pltpu.VMEM((2, nreq, tile), jnp.int32),
            pltpu.VMEM((2, nreq, tile), F32),
            pltpu.VMEM((nb, tile), F32),
            pltpu.VMEM((nb, tile), F32),
            pltpu.VMEM((allrows, tile), F32),
            pltpu.VMEM((tiles * slots, tile), F32),
            pltpu.VMEM(((1 + pools) * nclass, tile), F32),
            sem((10,)),
            sem((n_s,)),
            sem((n_s,)),
            sem((n_s,)),
            sem((n_s,)),
            sem((n_m,)),
            sem((n_m,)),
            sem((n_m,)),
            sem((n_m,)),
            sem((n_s,)),
            sem((n_s,)),
            sem((stage, n_m)),
            sem((stage, n_m)),
        ],
        compiler_params=pltpu.CompilerParams(
            collective_id=0, has_side_effects=True, vmem_limit_bytes=24 * 1024 * 1024
        ),
        cost_estimate=pl.CostEstimate(
            flops=2 * blocks * tile * (allrows + nreq), bytes_accessed=2 * blocks * tile, transcendentals=4 * nreq * tile
        ),
        name="inversion",
    )(
        pinned(sensitivity_blocks.reshape(blocks, tile)),
        pinned(block_placement_table),
        pinned(needed_tile_lists.T),
        pinned(location_category.reshape(tiles, tile)),
        pinned(ground_warmth_celsius),
        pinned(wetness_factor),
        pinned(carbon_reservoirs),
        category_sensitivity_effect,
        reservoir_decay_effect,
        pinned(category_sensitivity_effect.reshape(1, nclass)),
        pinned(reservoir_decay_effect),
        pinned(measured_anomaly),
        pinned(retrieval_precision),
    )
    model, grad, classes, cost = pl.pallas_call(
        hand_over,
        out_shape=results,
        in_specs=[vmem] * 4,
        out_specs=(hbm,) * 4,
        scratch_shapes=[sem((4,))],
        compiler_params=pltpu.CompilerParams(vmem_limit_bytes=2 * 1024 * 1024),
        name="results",
    )(*outs)
    return model, grad, classes, cost.reshape(())


def solution(mesh):
    in_specs = (
        P(("snd", "map"), None, None),
        P(None, ("snd", "map")),
        P(("snd", "map"), None),
        P("map"),
        P("snd", "map"),
        P("snd", "map"),
        P(None, "map"),
        P(),
        P(),
        P(("snd", "map"), None),
        P(("snd", "map"), None),
    )
    out_specs = (P(("snd", "map"), None), P("snd", "map"), P(), P())
    return jax.shard_map(
        functools.partial(shards, mesh.shape["snd"], mesh.shape["map"]),
        mesh=mesh,
        in_specs=in_specs,
        out_specs=out_specs,
        check_vma=False,
    )
```
